256 devices in a mesh: dp: 64 (over y, z, core), grp: 4 (over x).
Axes of the slice: x: 4, y: 4, z: 8, core: 2. Of those that a mesh axis runs over, the one named last changes fastest.
Arguments:
- states: bfloat16 [32768, 1024], P('dp'), may hold values from -8 to 8
- w_up: bfloat16 [1024, 4096], P('dp', 'grp'), may hold values from -0.1875 to 0.1875
- w_down: bfloat16 [4096, 1024], P('grp', 'dp'), may hold values from -0.09375 to 0.09375
- gain: float32 [1024], replicated, may hold values from 0.5 to 1.5
- query_lengths: int32 [64, 8], P('dp'), may hold values from 1 to 32, as said below
- passage_lengths: int32 [64, 8], P('dp'), may hold values from 1 to 128, as said below
- positive: int32 [512], P('dp'), may hold values from 0 to 511, as said below
- negatives: int32 [512, 15], P('dp'), may hold values from 0 to 511
Outputs:
- loss: float32 [], replicated
- grad_up: float32 [1024, 4096], P('dp', 'grp')
- grad_down: float32 [4096, 1024], P('grp', 'dp')
- grad_gain: float32 [1024], replicated
The draws below stay inside these ranges and needn't reach their ends.
Inputs may be any that keep to these rules, and one draw needn't show every extreme that they name: `query_lengths`: each row sums to 128. `passage_lengths`: each row sums to 384. Every passage is the positive of exactly one query, and it is held on a dp index other than that query's own. `negatives`: ids may repeat.
All inputs are finite; a program needn't handle non-finite values.
Results may differ from the reference program's by a relative error of at most 0.0029.
Values may be sent and summed in bfloat16 or wider, within the bound.
No kernel may reach another device: no remote copies, remote signals or barrier semaphores. Data moves between devices by JAX's collectives and lax.ppermute only.
A program may use at most 64 MiB of HBM per device.

```python
import math
import jax
import jax.numpy as jnp
import numpy as np
from jax import lax

MODEL_WIDTH = 1024
FF = 4096
NEG = 15
QUERY_SHARD = 8
PASSAGE_SHARD = 8
QTOK = 128
PTOK = 384
TOK_DEV = 512
TOKENS = 32768
QUERY_TOTAL = 512
PASSAGE_TOTAL = 512
N_DP = 64


kinship = 0.31


kinship_rest = 0.9507


topic_weight = 0.8944272


noise_weight = 0.4472136


def spread_lengths(key, row_count, columns, row_total, largest):
    others = columns - 1
    spare_units = row_total - largest - others
    slot_ids = jnp.arange(others, dtype=jnp.int32)
    even_share = spare_units // others + (slot_ids < spare_units % others).astype(jnp.int32)
    extras = jnp.broadcast_to(even_share[None, :], (row_count, others)).astype(jnp.int32)
    key_list = jax.random.split(key, 2 + 3 * others)
    key_count = 0
    for passes in range(3):
        for first_slot in range(passes % 2, others - 1, 2):
            upper_share = extras[:, first_slot]
            lower_share = extras[:, first_slot + 1]
            floor_move = jnp.maximum(-lower_share, upper_share - (largest - 1))
            ceil_move = jnp.minimum(upper_share, largest - 1 - lower_share)
            transfer = jax.random.randint(key_list[key_count], (row_count,), floor_move, ceil_move + 1, dtype=jnp.int32)
            key_count = key_count + 1
            extras = extras.at[:, first_slot].add(-transfer).at[:, first_slot + 1].add(transfer)
    peak_slot = jax.random.randint(key_list[key_count], (row_count, 1), 0, columns, dtype=jnp.int32)
    positions = jnp.arange(columns, dtype=jnp.int32)[None, :]
    source = jnp.clip(positions - (positions > peak_slot).astype(jnp.int32), 0, others - 1)
    picked = jnp.take_along_axis(extras, jnp.broadcast_to(source, (row_count, columns)), axis=1)
    return jnp.where(positions == peak_slot, largest, 1 + picked).astype(jnp.int32)


def device_cycle(sub_key):
    return jax.random.permutation(sub_key, N_DP)


def slot_cycle(sub_key):
    return jax.random.permutation(sub_key, PASSAGE_SHARD)


def layout(key):
    query_key, passage_key, device_key, slot_key = jax.random.split(key, 4)
    query_lens = spread_lengths(query_key, N_DP, QUERY_SHARD, QTOK, QTOK // 4)
    passage_lens = spread_lengths(passage_key, N_DP, PASSAGE_SHARD, PTOK, PTOK // 3)
    device_orders = jax.vmap(device_cycle)(jax.random.split(device_key, QUERY_SHARD)).astype(jnp.int32)
    slot_rows = jnp.arange(QUERY_SHARD, dtype=jnp.int32)[:, None]
    devices = jnp.arange(N_DP, dtype=jnp.int32)
    places = jnp.zeros((QUERY_SHARD, N_DP), jnp.int32).at[slot_rows, device_orders].set(jnp.broadcast_to(devices[None, :], (QUERY_SHARD, N_DP)))
    target = jnp.take_along_axis(device_orders, (places + 1) % N_DP, axis=1)
    slot_orders = jax.vmap(slot_cycle)(jax.random.split(slot_key, N_DP)).astype(jnp.int32)
    destination = target.T
    slot_index = slot_orders[destination, jnp.arange(QUERY_SHARD, dtype=jnp.int32)[None, :]]
    positive = (destination * PASSAGE_SHARD + slot_index).reshape(QUERY_TOTAL).astype(jnp.int32)
    return (query_lens, passage_lens, positive)


def draw_query_lengths(key, part):
    return layout(key)[0]


def draw_passage_lengths(key, part):
    return layout(key)[1]


def draw_positive(key, part):
    return layout(key)[2]


def draw_states(key, part):
    query_lens, passage_lens, positive = layout(key)
    key = jax.random.fold_in(key, 11)
    topic_key, fresh_key, noise_key, pair_key = jax.random.split(key, 4)
    topic_query = jnp.clip(jax.random.normal(topic_key, (QUERY_TOTAL, MODEL_WIDTH), jnp.float32), -6.0, 6.0)
    topic_fresh = jnp.clip(jax.random.normal(fresh_key, (PASSAGE_TOTAL, MODEL_WIDTH), jnp.float32), -6.0, 6.0)
    token_noise = jnp.clip(jax.random.normal(noise_key, (N_DP, TOK_DEV, MODEL_WIDTH), jnp.float32), -6.0, 6.0)
    owner_query = jnp.zeros((PASSAGE_TOTAL,), jnp.int32).at[positive].set(jnp.arange(QUERY_TOTAL, dtype=jnp.int32))
    passage_topic = kinship * topic_query[owner_query] + kinship_rest * topic_fresh
    sequence_topics = jnp.concatenate([topic_query.reshape(N_DP, QUERY_SHARD, MODEL_WIDTH), passage_topic.reshape(N_DP, PASSAGE_SHARD, MODEL_WIDTH)], axis=1)
    positions = jnp.arange(TOK_DEV, dtype=jnp.int32)[None, :, None]
    query_ends = jnp.cumsum(query_lens, axis=1)[:, None, :]
    passage_ends = jnp.cumsum(passage_lens, axis=1)[:, None, :]
    query_ids = jnp.sum((positions >= query_ends).astype(jnp.int32), axis=2)
    passage_ids = QUERY_SHARD + jnp.sum((positions - QTOK >= passage_ends).astype(jnp.int32), axis=2)
    sequence_ids = jnp.where(positions[:, :, 0] < QTOK, query_ids, passage_ids).astype(jnp.int32)
    token_topic = jnp.take_along_axis(sequence_topics, sequence_ids[:, :, None], axis=1)
    pairing = jax.random.permutation(pair_key, N_DP).astype(jnp.int32)
    block_ids = jnp.arange(MODEL_WIDTH, dtype=jnp.int32) // (MODEL_WIDTH // N_DP)
    spike_factor = jnp.where(block_ids[None, :] == pairing[:, None], 2.0, 1.0).astype(jnp.float32)
    values = 0.5 * (topic_weight * token_topic + noise_weight * token_noise) * spike_factor[:, None, :]
    return jnp.clip(values, -8.0, 8.0).reshape(TOKENS, MODEL_WIDTH).astype(jnp.bfloat16)


def place_ends(array, own_key, low, top_value):
    dims = array.shape
    index_at = [jax.random.randint(jax.random.fold_in(own_key, axis), (), 0, dims[axis]) for axis in range(len(dims))]
    array = array.at[tuple(index_at)].set(low)
    longest = dims.index(max(dims))
    index_at[longest] = (index_at[longest] + 1) % dims[longest]
    return array.at[tuple(index_at)].set(top_value)


def block_levels(stream_key, extent, cuts, smallest, high):
    level = 1.0
    for dim, blocks in cuts:
        draws = jax.random.uniform(jax.random.fold_in(jax.random.fold_in(stream_key, 6), dim), (blocks,), jnp.float32, smallest / len(cuts), high / len(cuts))
        level = level * jnp.repeat(jnp.exp(draws), extent[dim] // blocks).reshape((-1,) + (1,) * (len(extent) - 1 - dim))
    return level


def rank_bounds(amount, skew):
    weights = [(1 << 20) // math.isqrt(rank ** skew) + 1 for rank in range(1, amount + 1)]
    scale = 1 + sum(weights) // (1 << 30)
    return np.cumsum(np.array([max(1, weight // scale) for weight in weights]))


def ranked(key, shape, count, skew):
    table = rank_bounds(count, skew)
    pick = jax.random.randint(jax.random.fold_in(key, 1), shape, 0, int(table[count - 1]))
    grade = jnp.searchsorted(jnp.asarray(table, jnp.int32), pick, side="right")
    return jax.random.permutation(jax.random.fold_in(key, 2), count)[grade].astype(jnp.int32)


def gaussian(stream_key, shape, scale, most, cuts=(), kind=jnp.bfloat16):
    array = scale * jax.random.normal(stream_key, shape, jnp.float32)
    if cuts:
        array = array * block_levels(stream_key, shape, cuts, -0.22, 0.18)
    return jnp.clip(array, -most, most).astype(kind)


def setup_inputs(seed: int = 0) -> dict:
    keys = jax.random.split(jax.random.key(seed), 9)
    states = draw_states(jax.random.fold_in(keys[8], 71), 0)
    w_up = gaussian(keys[1], (MODEL_WIDTH, FF), MODEL_WIDTH ** -0.5, 0.1875, ((0, 64), (1, 4)))
    w_down = gaussian(keys[2], (FF, MODEL_WIDTH), FF ** -0.5, 0.09375, ((0, 4), (1, 64)))
    gain = jnp.clip(1.0 + 0.1 * jax.random.normal(keys[3], (MODEL_WIDTH,), jnp.float32), 0.5, 1.5)
    query_lengths = draw_query_lengths(jax.random.fold_in(keys[8], 71), 0)
    passage_lengths = draw_passage_lengths(jax.random.fold_in(keys[8], 71), 0)
    positive = draw_positive(jax.random.fold_in(keys[8], 71), 0)
    negatives = place_ends(ranked(keys[7], (QUERY_TOTAL, NEG), PASSAGE_TOTAL, 2), jax.random.fold_in(keys[7], 3), 0, PASSAGE_TOTAL - 1).astype(jnp.int32)
    return dict(states=states, w_up=w_up, w_down=w_down, gain=gain, query_lengths=query_lengths, passage_lengths=passage_lengths, positive=positive, negatives=negatives)


softmax_temper = 0.02
exact_precision = lax.Precision.HIGHEST

def normal_cdf(values):
    return 0.5 * (1.0 + lax.erf(values * 0.7071067811865476))

def gelu_exact(values):
    return values * normal_cdf(values)

def gelu_slope(values):
    return normal_cdf(values) + values * jnp.exp(-0.5 * values * values) * 0.3989422804014327

def segment_table(query_lengths, passage_lengths, total):
    query_starts = jnp.cumsum(query_lengths) - query_lengths
    passage_starts = QTOK + jnp.cumsum(passage_lengths) - passage_lengths
    starts = jnp.concatenate([query_starts, passage_starts]).astype(jnp.int32)
    lengths = jnp.concatenate([query_lengths, passage_lengths]).astype(jnp.int32)
    places = jnp.arange(total, dtype=jnp.int32)[:, None]
    inside = (places >= starts[None, :]) & (places < (starts + lengths)[None, :])
    return inside.astype(jnp.float32) / lengths.astype(jnp.float32)[None, :]

def norm_pool(mixed, gain, table):
    middle = lax.optimization_barrier(jnp.mean(mixed, axis=-1, keepdims=True))
    centred = mixed - middle
    inverse = lax.rsqrt(lax.optimization_barrier(jnp.mean(centred * centred, axis=-1, keepdims=True)) + 1e-05)
    normed = centred * inverse
    output = normed * gain[None, :]
    pooled = lax.dot_general(table, output, (((0,), (0,)), ((), ())), precision=exact_precision)
    scale = lax.rsqrt(lax.optimization_barrier(jnp.sum(pooled * pooled, axis=-1, keepdims=True)) + 1e-06)
    return (inverse, normed, scale, pooled * scale)

def norm_back(d_embed, embed, scale, table, inverse, normed, gain):
    d_pooled = scale * (d_embed - embed * lax.optimization_barrier(jnp.sum(embed * d_embed, axis=-1, keepdims=True)))
    d_out = jnp.dot(table, d_pooled, precision=exact_precision)
    d_gain = lax.optimization_barrier(jnp.sum(d_out * normed, axis=0))
    d_normed = d_out * gain[None, :]
    d_mixed = inverse * (d_normed - lax.optimization_barrier(jnp.mean(d_normed, axis=-1, keepdims=True)) - normed * lax.optimization_barrier(jnp.mean(d_normed * normed, axis=-1, keepdims=True)))
    return (d_gain, d_mixed.astype(jnp.bfloat16))

def block_forward(block, w_up, w_down, gain, table):
    upward = jnp.dot(block, w_up, preferred_element_type=jnp.float32)
    hidden = gelu_exact(upward).astype(jnp.bfloat16)
    mixed = block.astype(jnp.float32) + jnp.dot(hidden, w_down, preferred_element_type=jnp.float32)
    inverse, normed, scale, embed = norm_pool(mixed, gain, table)
    return (upward, hidden, inverse, normed, scale, embed)

def reference(states, w_up, w_down, gain, query_lengths, passage_lengths, positive, negatives):
    blocks = states.reshape(N_DP, TOK_DEV, MODEL_WIDTH)

    def embed_block(inputs):
        block, q_lens, p_lens = inputs
        table = segment_table(q_lens, p_lens, TOK_DEV)
        return block_forward(block, w_up, w_down, gain, table)[5]
    embeds = lax.map(embed_block, (blocks, query_lengths, passage_lengths))
    query_block_list = embeds[:, :QUERY_SHARD]
    passage_block_list = embeds[:, QUERY_SHARD:]
    query_rows = query_block_list.reshape(QUERY_TOTAL, MODEL_WIDTH)
    passages = passage_block_list.reshape(PASSAGE_TOTAL, MODEL_WIDTH)
    listed = jnp.concatenate([positive[:, None], negatives], axis=1).astype(jnp.int32)
    chosen_rows = passages[listed]
    remote_shard = jnp.einsum('za,zea->ze', query_rows, chosen_rows, precision=exact_precision) / softmax_temper
    local_shard = jnp.einsum('nwu,nvu->nwv', query_block_list, passage_block_list, precision=exact_precision)
    local_shard = local_shard.reshape(QUERY_TOTAL, PASSAGE_SHARD) / softmax_temper
    logits = jnp.concatenate([remote_shard, local_shard], axis=1)
    top = lax.optimization_barrier(jnp.max(logits, axis=1, keepdims=True))
    weights = jnp.exp(logits - top)
    total = lax.optimization_barrier(jnp.sum(weights, axis=1, keepdims=True))
    each = jnp.log(total[:, 0]) + top[:, 0] - logits[:, 0]
    loss = jnp.mean(each)
    first = (jnp.arange(NEG + 1 + PASSAGE_SHARD, dtype=jnp.int32) == 0).astype(jnp.float32)
    d_logits = weights / total - first[None, :]
    remote_weight = d_logits[:, :NEG + 1]
    local_weight = d_logits[:, NEG + 1:]
    local_query_rows = jnp.einsum('tsn,tnw->tsw', local_weight.reshape(N_DP, QUERY_SHARD, PASSAGE_SHARD), passage_block_list, precision=exact_precision)
    query_gradient = (jnp.einsum('hu,hup->hp', remote_weight, chosen_rows, precision=exact_precision) + local_query_rows.reshape(QUERY_TOTAL, MODEL_WIDTH)) / softmax_temper
    share_term = remote_weight[:, :, None] * query_rows[:, None, :] / softmax_temper
    passage_gradient = jnp.zeros((PASSAGE_TOTAL, MODEL_WIDTH), jnp.float32).at[listed.reshape(-1)].add(share_term.reshape(-1, MODEL_WIDTH))
    local_passage_rows = jnp.einsum('lje,ljn->len', local_weight.reshape(N_DP, QUERY_SHARD, PASSAGE_SHARD), query_block_list, precision=exact_precision)
    passage_gradient = passage_gradient + local_passage_rows.reshape(PASSAGE_TOTAL, MODEL_WIDTH) / softmax_temper
    d_blocks = jnp.concatenate([query_gradient.reshape(N_DP, QUERY_SHARD, MODEL_WIDTH), passage_gradient.reshape(N_DP, PASSAGE_SHARD, MODEL_WIDTH)], axis=1)

    def back_step(carry, inputs):
        sum_up, sum_down, sum_gain = carry
        block, q_lens, p_lens, d_embed = inputs
        table = segment_table(q_lens, p_lens, TOK_DEV)
        upward, hidden, inverse, normed, scale, embed = block_forward(block, w_up, w_down, gain, table)
        d_gain, d_mixed = norm_back(d_embed, embed, scale, table, inverse, normed, gain)
        sum_down = sum_down + lax.dot_general(hidden, d_mixed, (((0,), (0,)), ((), ())), preferred_element_type=jnp.float32)
        d_hidden = lax.dot_general(d_mixed, w_down, (((1,), (1,)), ((), ())), preferred_element_type=jnp.float32)
        d_upward = (d_hidden * gelu_slope(upward)).astype(jnp.bfloat16)
        sum_up = sum_up + lax.dot_general(block, d_upward, (((0,), (0,)), ((), ())), preferred_element_type=jnp.float32)
        return ((sum_up, sum_down, sum_gain + d_gain), None)
    start = (jnp.zeros((MODEL_WIDTH, FF), jnp.float32), jnp.zeros((FF, MODEL_WIDTH), jnp.float32), jnp.zeros((MODEL_WIDTH,), jnp.float32))
    (grad_up, grad_down, grad_gain), unused = lax.scan(back_step, start, (blocks, query_lengths, passage_lengths, d_blocks))
    return (loss, grad_up, grad_down, grad_gain)
```

```python
import jax
import jax.numpy as jnp
from jax import lax
from jax.sharding import Mesh, PartitionSpec as P

QTOK = 128
Y, Z, CORE, GRP = 4, 8, 2, 4
TEMPER = 0.02
EMBED_STEP = 1024.0
PARTIAL_STEP = 0.25
f32, bf16, f16 = jnp.float32, jnp.bfloat16, jnp.float16
EXACT = lax.Precision.HIGHEST
THREE = lax.Precision.HIGH


def normal_cdf(values):
    return 0.5 * (1.0 + lax.erf(values * 0.7071067811865476))


def gelu_exact(values):
    return values * normal_cdf(values)


def gelu_slope(values):
    return normal_cdf(values) + values * jnp.exp(-0.5 * values * values) * 0.3989422804014327


def segment_table(query_lengths, passage_lengths, total):
    query_starts = jnp.cumsum(query_lengths) - query_lengths
    passage_starts = QTOK + jnp.cumsum(passage_lengths) - passage_lengths
    starts = jnp.concatenate([query_starts, passage_starts])
    lengths = jnp.concatenate([query_lengths, passage_lengths])
    places = jnp.arange(total, dtype=jnp.int32)[:, None]
    inside = (places >= starts[None, :]) & (places < (starts + lengths)[None, :])
    return inside.astype(f32) / lengths.astype(f32)[None, :]


def spread(value, axis, count):
    return lax.all_to_all(jnp.broadcast_to(value[None], (count,) + value.shape), axis, 0, 0)


def other_core(value):
    return lax.ppermute(value, "core", [(0, 1), (1, 0)])


def shifted(value, axis, count, step):
    return lax.ppermute(value, axis, [(j, (j + step) % count) for j in range(count)])


def sum_permutes(value, axis, count):
    place = lax.axis_index(axis)
    moved = jnp.stack([value] + [shifted(value, axis, count, k) for k in range(1, count)])
    total = lax.dynamic_index_in_dim(moved, place, 0, keepdims=False)
    for k in range(1, count):
        total = total + lax.dynamic_index_in_dim(moved, (place - k) % count, 0, keepdims=False)
    return total


def scatter_permutes(value, axis, count):
    place = lax.axis_index(axis)
    pieces = value.reshape((count, value.shape[0] // count) + value.shape[1:])
    total = lax.dynamic_index_in_dim(pieces, place, 0, keepdims=False)
    moved = []
    for k in range(1, count):
        piece = lax.dynamic_index_in_dim(pieces, (place + k) % count, 0, keepdims=False)
        moved.append(shifted(piece.astype(bf16), axis, count, k))
    for piece in moved:
        total = total + piece.astype(f32)
    return total


def scatter_exchange(value, axis, count):
    pieces = value.astype(bf16).reshape((count, value.shape[0] // count) + value.shape[1:])
    return jnp.sum(lax.all_to_all(pieces, axis, 0, 0).astype(f32), axis=0)


def scatter_scaled(pieces, axis):
    width = pieces.shape[-1]
    largest = jnp.max(jnp.abs(pieces), axis=-1, keepdims=True)
    exponent = jnp.floor(jnp.log2(jnp.maximum(largest, 1e-30)))
    scaled = pieces * jnp.exp2(-exponent)
    lanes = jnp.broadcast_to(exponent, pieces.shape[:-1] + (128,))
    moved = lax.all_to_all(jnp.concatenate([scaled, lanes], axis=-1).astype(f16), axis, 0, 0)
    return jnp.sum(moved[..., :width].astype(f32) * jnp.exp2(moved[..., width : width + 1].astype(f32)), axis=0)


def dot_nt(a, b, precision=None):
    return lax.dot_general(
        a, b, (((1,), (1,)), ((), ())), precision=precision, preferred_element_type=f32
    )


def dot_tn(a, b, precision=None):
    return lax.dot_general(
        a, b, (((0,), (0,)), ((), ())), precision=precision, preferred_element_type=f32
    )


def shards(states, w_up, w_down, gain, query_lengths, passage_lengths, positive, negatives):
    tokens, width = states.shape
    half = width // 2
    owned = w_up.shape[0]
    quarter = tokens // GRP
    queries = positive.shape[0]
    core = lax.axis_index("core")
    member = lax.axis_index("grp")
    block = core * (Y * Z) + lax.axis_index("y") * Z + lax.axis_index("z")

    def swap_halves(value):
        return jnp.where(core == 0, value, jnp.roll(value, half, axis=-1))

    cores = states.reshape(tokens, Y * Z, CORE, owned).transpose(2, 0, 1, 3).reshape(CORE, tokens, half)
    states_mine = lax.dynamic_index_in_dim(cores, core, 0, keepdims=False)
    states_theirs = lax.dynamic_index_in_dim(cores, 1 - core, 0, keepdims=False)
    gain_common = gain.reshape(Y * Z, CORE, owned).transpose(1, 0, 2).reshape(1, width)
    gain_local = swap_halves(gain_common)

    both = jnp.stack([w_up, w_down.T])
    along_z = spread(both, "z", Z).transpose(1, 0, 2, 3)
    along_z, states_mine, states_theirs = lax.optimization_barrier((along_z, states_mine, states_theirs))
    along_y = spread(along_z, "y", Y)
    up_mine = along_y[:, 0].reshape(half, -1)
    down_mine = along_y[:, 1].reshape(half, -1)
    up_theirs = other_core(up_mine)
    down_theirs = other_core(down_mine)
    states_sent = other_core(states_theirs)

    upward = jnp.dot(states_mine, up_mine, preferred_element_type=f32) + jnp.dot(
        states_theirs, up_theirs, preferred_element_type=f32
    )
    hidden = gelu_exact(upward).astype(bf16)
    hidden_sent = other_core(hidden)
    partial = jnp.concatenate([dot_nt(hidden, down_mine), dot_nt(hidden, down_theirs)], axis=1)

    arrived = lax.all_to_all((partial * PARTIAL_STEP).astype(f16).reshape(GRP, quarter, width), "grp", 0, 0)
    states_local = jnp.concatenate([states_mine, states_theirs], axis=1)
    states_quarter = lax.dynamic_slice_in_dim(states_local, member * quarter, quarter, 0)
    mixed = states_quarter.astype(f32) + jnp.sum(arrived.astype(f32), axis=0) * (1.0 / PARTIAL_STEP)
    centred = mixed - jnp.mean(mixed, axis=-1, keepdims=True)
    inverse = lax.rsqrt(jnp.mean(centred * centred, axis=-1, keepdims=True) + 1e-05)
    normed = centred * inverse
    table = segment_table(query_lengths[0], passage_lengths[0], tokens)
    table_quarter = lax.dynamic_slice_in_dim(table, member * quarter, quarter, 0)
    pooled = sum_permutes(dot_tn(table_quarter, normed, EXACT), "grp", GRP) * gain_local
    scale = lax.rsqrt(jnp.sum(pooled * pooled, axis=-1, keepdims=True) + 1e-06)
    embed = pooled * scale

    centred_sent = centred.astype(bf16)
    centred_all = lax.all_gather(centred_sent, "grp", axis=0, tiled=True)

    listed = jnp.concatenate([positive[:, None], negatives], axis=1)
    owner = listed // queries
    listed = ((owner % CORE) * (Y * Z) + owner // CORE) * queries + listed % queries
    lanes = jnp.pad(listed.astype(f32), ((0, queries), (0, 128 - listed.shape[1])))
    sent = jnp.concatenate([swap_halves(embed) * EMBED_STEP, lanes], axis=1).astype(f16)
    mine = spread(spread(sent, "z", Z), "y", Y)
    theirs = other_core(mine)
    first = jnp.where(core == 0, mine, theirs)
    second = jnp.where(core == 0, theirs, mine)
    gathered = jnp.stack([first, second]).reshape(CORE * Y * Z, 2 * queries, width + 128)
    ids = gathered[:, :queries, width : width + listed.shape[1]].astype(jnp.int32)
    ids = ids.reshape(-1, listed.shape[1])
    embeds = gathered[:, :, :width].astype(f32) * (1.0 / EMBED_STEP)
    all_queries = embeds[:, :queries].reshape(-1, width)
    all_passages = embeds[:, queries:].reshape(-1, width)

    count = all_queries.shape[0]
    ids = ids.T
    places = lax.broadcasted_iota(jnp.int32, (count, count), 0)
    columns = lax.broadcasted_iota(jnp.int32, (count, count), 1)
    is_first = (places == ids[:1]).astype(f32)
    times = is_first + (places // queries == columns // queries).astype(f32)
    for k in range(1, listed.shape[1]):
        times = times + (places == ids[k : k + 1]).astype(f32)
    logits = dot_nt(all_passages, all_queries, THREE) / TEMPER
    named = times > 0
    top = jnp.max(jnp.where(named, logits, -jnp.inf), axis=0, keepdims=True)
    weights = times * jnp.exp(jnp.where(named, logits - top, 0.0))
    total = jnp.sum(weights, axis=0, keepdims=True)
    each = jnp.log(total) + top - jnp.sum(is_first * logits, axis=0, keepdims=True)
    loss = jnp.mean(each)
    d_logits = weights / total - is_first

    own_passages = lax.dynamic_slice_in_dim(d_logits, block * queries, queries, 0)
    own_queries = lax.dynamic_slice_in_dim(d_logits, block * queries, queries, 1)
    d_embed = jnp.concatenate(
        [
            dot_tn(own_queries, all_passages, THREE),
            jnp.dot(own_passages, all_queries, precision=THREE),
        ],
        axis=0,
    ) / TEMPER
    d_embed = swap_halves(d_embed)

    d_pooled = scale * (d_embed - embed * jnp.sum(embed * d_embed, axis=-1, keepdims=True))
    centred_all = centred_all.astype(f32)
    inverse_all = lax.rsqrt(jnp.mean(centred_all * centred_all, axis=-1, keepdims=True) + 1e-05)
    normed_all = centred_all * inverse_all
    d_normed = jnp.dot(table, d_pooled * gain_local, precision=EXACT)
    d_mixed = inverse_all * (
        d_normed
        - jnp.mean(d_normed, axis=-1, keepdims=True)
        - normed_all * jnp.mean(d_normed * normed_all, axis=-1, keepdims=True)
    )
    d_mixed = d_mixed.astype(bf16)
    d_mine, d_theirs = d_mixed[:, :half], d_mixed[:, half:]

    d_sent = other_core(d_theirs)
    down_half = dot_tn(d_mine, hidden) + dot_tn(d_sent, hidden_sent)
    down_rows = scatter_permutes(down_half, "y", Y)
    d_hidden = jnp.dot(d_mine, down_mine, preferred_element_type=f32) + jnp.dot(
        d_theirs, down_theirs, preferred_element_type=f32
    )
    d_upward = (d_hidden * gelu_slope(upward)).astype(bf16)
    up_half = dot_tn(states_mine, d_upward) + dot_tn(states_sent, other_core(d_upward))
    up_rows = scatter_exchange(up_half, "y", Y)
    last = jnp.concatenate(
        [up_rows.reshape(Z, owned, -1), down_rows.reshape(Z, owned, -1)], axis=1
    )
    last = scatter_scaled(last, "z")
    grad_up = last[:owned]
    grad_down = last[owned:].T

    d_logits, down_half = lax.optimization_barrier((d_logits, down_half))
    pulled = d_logits * logits
    product = jnp.sum(jnp.dot(d_logits, all_queries, precision=THREE) * all_passages, axis=0)
    grad_gain = (
        (2.0 / TEMPER) * product
        - jnp.sum(jnp.sum(pulled, axis=0)[:, None] * all_queries * all_queries, axis=0)
        - jnp.sum(jnp.sum(pulled, axis=1)[:, None] * all_passages * all_passages, axis=0)
    ) / gain_common[0]
    grad_gain = grad_gain.reshape(CORE, Y * Z, owned).transpose(1, 0, 2).reshape(width)
    return (loss, grad_up, grad_down, grad_gain)


def solution(mesh):
    split = Mesh(mesh.devices.reshape(Y, Z, CORE, GRP), ("y", "z", "core", "grp"))
    dp = ("y", "z", "core")
    return jax.shard_map(
        shards,
        mesh=split,
        in_specs=(
            P(dp, None),
            P(dp, "grp"),
            P("grp", dp),
            P(),
            P(dp, None),
            P(dp, None),
            P(dp),
            P(dp, None),
        ),
        out_specs=(P(), P(dp, "grp"), P("grp", dp), P()),
        check_vma=False,
    )
```

```python
import functools

import jax
import jax.numpy as jnp
from jax import lax
from jax.experimental import pallas as pl
from jax.experimental.pallas import tpu as pltpu
from jax.sharding import Mesh, PartitionSpec as P

QTOK = 128
Y, Z, CORE, GRP = 4, 8, 2, 4
TEMPER = 0.02
EMBED_STEP = 1024.0
PARTIAL_STEP = 0.25
f32, bf16, f16 = jnp.float32, jnp.bfloat16, jnp.float16
EXACT = lax.Precision.HIGHEST
THREE = lax.Precision.HIGH


def normal_cdf(values):
    return 0.5 * (1.0 + lax.erf(values * 0.7071067811865476))


def gelu_exact(values):
    return values * normal_cdf(values)


def gelu_slope(values):
    return normal_cdf(values) + values * jnp.exp(-0.5 * values * values) * 0.3989422804014327


def segment_table(query_lengths, passage_lengths, total, shift):
    query_starts = jnp.cumsum(query_lengths) - query_lengths
    passage_starts = QTOK + jnp.cumsum(passage_lengths) - passage_lengths
    starts = jnp.concatenate([query_starts, passage_starts])
    lengths = jnp.concatenate([query_lengths, passage_lengths])
    places = ((jnp.arange(total, dtype=jnp.int32) + shift) % total)[:, None]
    inside = (places >= starts[None, :]) & (places < (starts + lengths)[None, :])
    return inside.astype(f32) / lengths.astype(f32)[None, :]


def spread(value, axis, count):
    return lax.all_to_all(jnp.broadcast_to(value[None], (count,) + value.shape), axis, 0, 0)


def other_core(value):
    return lax.ppermute(value, "core", [(0, 1), (1, 0)])


def shifted(value, axis, count, step):
    return lax.ppermute(value, axis, [(j, (j + step) % count) for j in range(count)])


def send_shifted(value, axis, count):
    return [shifted(value, axis, count, k) for k in range(1, count)]


def place_kernel(place, *refs):
    *pieces, out = refs
    count = len(pieces)
    for k, piece in enumerate(pieces):
        out[lax.rem(place[0] + count - k, count)] = piece[...]


def place_pieces(value, moved, axis):
    pieces = [value, *moved]
    vmem = pl.BlockSpec(memory_space=pltpu.VMEM)
    return pl.pallas_call(
        place_kernel,
        out_shape=jax.ShapeDtypeStruct((len(pieces),) + value.shape, value.dtype),
        in_specs=[pl.BlockSpec(memory_space=pltpu.SMEM)] + [vmem] * len(pieces),
        out_specs=vmem,
        compiler_params=pltpu.CompilerParams(vmem_limit_bytes=16 * 1024 * 1024),
        cost_estimate=pl.CostEstimate(flops=0, bytes_accessed=2**21, transcendentals=0),
    )(lax.axis_index(axis).reshape(1).astype(jnp.int32), *pieces)


def sum_permutes(value, axis, count):
    place = lax.axis_index(axis)
    moved = jnp.stack([value] + [shifted(value, axis, count, k) for k in range(1, count)])
    total = lax.dynamic_index_in_dim(moved, place, 0, keepdims=False)
    for k in range(1, count):
        total = total + lax.dynamic_index_in_dim(moved, (place - k) % count, 0, keepdims=False)
    return total


def scatter_scaled(pieces, axis):
    width = pieces.shape[-1]
    largest = jnp.max(jnp.abs(pieces), axis=-1, keepdims=True)
    exponent = jnp.floor(jnp.log2(jnp.maximum(largest, 1e-30)))
    scaled = pieces * jnp.exp2(-exponent)
    lanes = jnp.broadcast_to(exponent, pieces.shape[:-1] + (128,))
    moved = lax.all_to_all(jnp.concatenate([scaled, lanes], axis=-1).astype(f16), axis, 0, 0)
    return jnp.sum(moved[..., :width].astype(f32) * jnp.exp2(moved[..., width : width + 1].astype(f32)), axis=0)


def dot_nt(a, b, precision=None):
    return lax.dot_general(
        a, b, (((1,), (1,)), ((), ())), precision=precision, preferred_element_type=f32
    )


def dot_tn(a, b, precision=None):
    return lax.dot_general(
        a, b, (((0,), (0,)), ((), ())), precision=precision, preferred_element_type=f32
    )


def split_high(value):
    high = value.astype(bf16)
    return high, (value - high.astype(f32)).astype(bf16)


def three_nn(a, high, low):
    a_high, a_low = split_high(a)
    dot = functools.partial(jnp.dot, preferred_element_type=f32)
    return dot(a_high, high[...]) + (dot(a_high, low[...]) + dot(a_low, high[...]))


def loss_kernel(
    scalars, first, second, embed, scale, gain,
    d_logits, loss, d_sums, q_high, q_low, p_high, p_low, logits, times, ids,
):
    core, block = scalars[0], scalars[1]
    half_count = first.shape[0] * 8
    count, width = q_high.shape
    half = width // 2
    listed = ids.shape[0]

    def split(i, carry):
        for source, base in ((first, 0), (second, half_count)):
            rows = pl.ds(pl.multiple_of(base + 16 * i, 16), 16)
            for offset, high, low in ((0, q_high, q_low), (8, p_high, p_low)):
                value = source[pl.ds(2 * i, 2), offset : offset + 8, :width].reshape(16, width)
                high[rows, :], low[rows, :] = split_high(value)
        return carry

    lax.fori_loop(0, half_count // 16, split, 0)
    lanes = [source[:, 0:8, width:].reshape(half_count, 128) for source in (first, second)]
    ids[...] = jnp.concatenate(lanes, axis=0).T[:listed]

    to_logits = 1.0 / (TEMPER * EMBED_STEP * EMBED_STEP)
    raw = dot_nt(p_high[...], q_high[...])
    raw = raw + (dot_nt(p_high[...], q_low[...]) + dot_nt(p_low[...], q_high[...]))
    logits[...] = raw * to_logits

    step = 32
    columns = lax.broadcasted_iota(jnp.int32, (step, count), 1) >> 3
    offsets = lax.broadcasted_iota(jnp.int32, (step, count), 0)

    def fold(value):
        return value.reshape(step // 8, 8, count)

    def count_times(i, carry):
        top, named = carry
        rows = pl.ds(pl.multiple_of(i * step, step), step)
        places = offsets + i * step
        whole = places.astype(f32)
        is_first = whole == ids[0:1, :]
        total = jnp.where(is_first, 1.0, 0.0) + jnp.where((places >> 3) == columns, 1.0, 0.0)
        for k in range(1, listed):
            total = total + jnp.where(whole == ids[k : k + 1, :], 1.0, 0.0)
        value = logits[rows, :]
        times[rows, :] = total
        top = jnp.maximum(top, jnp.max(fold(jnp.where(total > 0.0, value, -1e30)), axis=0))
        return top, named + jnp.sum(fold(jnp.where(is_first, value, 0.0)), axis=0)

    start = (jnp.full((8, count), -1e30, f32), jnp.zeros((8, count), f32))
    top, named = lax.fori_loop(0, count // step, count_times, start)
    top = jnp.max(top, axis=0, keepdims=True)
    named = jnp.sum(named, axis=0, keepdims=True)

    def weigh(i, carry):
        rows = pl.ds(pl.multiple_of(i * step, step), step)
        total = times[rows, :]
        weight = total * jnp.exp(jnp.where(total > 0.0, logits[rows, :] - top, 0.0))
        times[rows, :] = weight
        return carry + jnp.sum(fold(weight), axis=0)

    total = lax.fori_loop(0, count // step, weigh, jnp.zeros((8, count), f32))
    total = jnp.sum(total, axis=0, keepdims=True)
    loss[...] = jnp.broadcast_to(
        jnp.sum(jnp.log(total) + top - named, axis=1, keepdims=True) / count, loss.shape
    )
    share = 1.0 / total

    def differ(i, carry):
        rows = pl.ds(pl.multiple_of(i * step, step), step)
        is_first = (offsets + i * step).astype(f32) == ids[0:1, :]
        d_logits[rows, :] = times[rows, :] * share - jnp.where(is_first, 1.0, 0.0)
        return carry

    lax.fori_loop(0, count // step, differ, 0)

    own_place = block * 8
    picks = lax.broadcasted_iota(jnp.int32, (16, count), 0)
    picks = (lax.broadcasted_iota(jnp.int32, (16, count), 1) == picks + own_place) & (picks < 8)
    picks = jnp.where(picks, 1.0, 0.0).astype(bf16)
    d_high, d_low = split_high(d_logits[...])
    own_queries = dot_nt(picks, d_high) + dot_nt(picks, d_low)
    own_passages = d_logits[pl.ds(pl.multiple_of(own_place, 8), 8), :]
    own_passages = jnp.concatenate([own_passages, jnp.zeros_like(own_passages)], axis=0)
    d_embed = jnp.concatenate(
        [
            three_nn(own_queries, p_high, p_low)[:8],
            three_nn(own_passages, q_high, q_low)[:8],
        ],
        axis=0,
    ) * (1.0 / (TEMPER * EMBED_STEP))
    turned = jnp.concatenate([d_embed[:, half:], d_embed[:, :half]], axis=1)
    d_embed = jnp.where(core == 0, d_embed, turned)
    owned = embed[...]
    inner = jnp.sum(owned * d_embed, axis=1, keepdims=True)
    d_sums[...] = scale[...] * (d_embed - owned * inner) * gain[...]


def back_kernel(
    d_sums, table, own, next1, next2, next3, d_mine, d_theirs, mine_turned, theirs_turned
):
    half = d_mine.shape[1]
    value_high, value_low = split_high(d_sums[...])
    dot = functools.partial(jnp.dot, preferred_element_type=f32)
    for k, source in enumerate((own, next1, next2, next3)):
        size = source.shape[0]
        places = slice(k * size, (k + 1) * size)
        centred = source[...].astype(f32)
        inverse = lax.rsqrt(jnp.mean(centred * centred, axis=1, keepdims=True) + 1e-05)
        normed = centred * inverse
        part_high, part_low = split_high(table[places, :])
        d_normed = dot(part_high, value_high) + (
            dot(part_high, value_low) + dot(part_low, value_high)
        )
        d_mixed = inverse * (
            d_normed
            - jnp.mean(d_normed, axis=1, keepdims=True)
            - normed * jnp.mean(d_normed * normed, axis=1, keepdims=True)
        )
        d_mine[places, :] = d_mixed[:, :half].astype(bf16)
        d_theirs[places, :] = d_mixed[:, half:].astype(bf16)
        mine_turned[:, places] = d_mixed[:, :half].T.astype(bf16)
        theirs_turned[:, places] = d_mixed[:, half:].T.astype(bf16)


def down_kernel(a, b, c, d, out):
    step = 128
    for row in range(0, a.shape[0], step):
        rows = slice(row, row + step)
        total = jnp.dot(a[rows, :], b[...], preferred_element_type=f32)
        total = total + jnp.dot(c[rows, :], d[...], preferred_element_type=f32)
        out[rows, :] = total.astype(bf16)


def both_kernel(a, b, c, d, ready, out):
    step = a.shape[1] // out.shape[0]
    for k in range(out.shape[0]):
        rows = slice(k * step, (k + 1) * step)
        out[k, 0] = (dot_tn(a[:, rows], b[...]) + dot_tn(c[:, rows], d[...])).astype(bf16)
        out[k, 1] = ready[rows, :]


def slope_kernel(a, b, c, d, slope, rounded):
    step = 128
    for row in range(0, a.shape[0], step):
        rows = slice(row, row + step)
        total = jnp.dot(a[rows, :], b[...], preferred_element_type=f32)
        total = total + jnp.dot(c[rows, :], d[...], preferred_element_type=f32)
        rounded[rows, :] = (total * slope[rows, :]).astype(bf16)


def pair_call(body, operands, shape):
    vmem = pl.BlockSpec(memory_space=pltpu.VMEM)
    return pl.pallas_call(
        body,
        out_shape=jax.ShapeDtypeStruct(shape, bf16),
        in_specs=[vmem] * len(operands),
        out_specs=vmem,
        compiler_params=pltpu.CompilerParams(vmem_limit_bytes=24 * 1024 * 1024),
        cost_estimate=pl.CostEstimate(flops=2**31, bytes_accessed=6 * 2**20, transcendentals=0),
    )(*operands)


def all_losses(scalars, first, second, embed, scale, gain, listed):
    count, width = first.shape[0] * 16, embed.shape[1]
    vmem = pl.BlockSpec(memory_space=pltpu.VMEM)
    return pl.pallas_call(
        loss_kernel,
        out_shape=(
            jax.ShapeDtypeStruct((count, count), f32),
            jax.ShapeDtypeStruct((8, 128), f32),
            jax.ShapeDtypeStruct(embed.shape, f32),
        ),
        in_specs=[pl.BlockSpec(memory_space=pltpu.SMEM)] + [vmem] * 5,
        out_specs=(vmem,) * 3,
        scratch_shapes=[pltpu.VMEM((count, width), bf16)] * 4
        + [pltpu.VMEM((count, count), f32)] * 2
        + [pltpu.VMEM((listed, count), f32)],
        compiler_params=pltpu.CompilerParams(vmem_limit_bytes=40 * 1024 * 1024),
        cost_estimate=pl.CostEstimate(flops=2**20, bytes_accessed=2**16, transcendentals=0),
    )(scalars, first, second, embed, scale, gain)


def norm_back(d_sums, table, quarters):
    tokens, half = table.shape[0], d_sums.shape[1] // 2
    vmem = pl.BlockSpec(memory_space=pltpu.VMEM)
    return pl.pallas_call(
        back_kernel,
        out_shape=(jax.ShapeDtypeStruct((tokens, half), bf16),) * 2
        + (jax.ShapeDtypeStruct((half, tokens), bf16),) * 2,
        in_specs=[vmem] * (2 + len(quarters)),
        out_specs=(vmem,) * 4,
        compiler_params=pltpu.CompilerParams(vmem_limit_bytes=24 * 1024 * 1024),
        cost_estimate=pl.CostEstimate(flops=2**20, bytes_accessed=2**16, transcendentals=0),
    )(d_sums, table, *quarters)


def shards(states, w_up, w_down, gain, query_lengths, passage_lengths, positive, negatives):
    tokens, width = states.shape
    half = width // 2
    owned = w_up.shape[0]
    quarter = tokens // GRP
    queries = positive.shape[0]
    core = lax.axis_index("core")
    member = lax.axis_index("grp")
    block = core * (Y * Z) + lax.axis_index("y") * Z + lax.axis_index("z")

    def swap_halves(value):
        return jnp.where(core == 0, value, jnp.roll(value, half, axis=-1))

    def turn(value):
        parts = value.reshape((GRP, quarter) + value.shape[1:])
        order = [lax.dynamic_index_in_dim(parts, (member + k) % GRP, 0, keepdims=False) for k in range(GRP)]
        return jnp.concatenate(order, axis=0)

    cores = turn(states).reshape(tokens, Y * Z, CORE, owned).transpose(2, 0, 1, 3).reshape(CORE, tokens, half)
    states_mine = lax.dynamic_index_in_dim(cores, core, 0, keepdims=False)
    states_theirs = lax.dynamic_index_in_dim(cores, 1 - core, 0, keepdims=False)
    gain_common = gain.reshape(Y * Z, CORE, owned).transpose(1, 0, 2).reshape(1, width)
    gain_local = swap_halves(gain_common)

    up_z = spread(w_up, "z", Z)
    up_z, states_mine, states_theirs, down_sent = lax.optimization_barrier(
        (up_z, states_mine, states_theirs, w_down.T)
    )
    down_z = spread(down_sent, "z", Z)
    up_moved = send_shifted(up_z, "y", Y)
    up_moved, down_z = lax.optimization_barrier((up_moved, down_z))
    up_mine = place_pieces(up_z, up_moved, "y").reshape(half, -1)
    up_theirs = other_core(up_mine)
    down_moved = send_shifted(down_z, "y", Y)
    states_sent = other_core(states_theirs)

    upward = jnp.dot(states_mine, up_mine, preferred_element_type=f32) + jnp.dot(
        states_theirs, up_theirs, preferred_element_type=f32
    )
    hidden = gelu_exact(upward).astype(bf16)
    hidden, down_moved = lax.optimization_barrier((hidden, down_moved))
    hidden_sent = other_core(hidden)
    down_mine = place_pieces(down_z, down_moved, "y").reshape(half, -1)
    down_theirs = other_core(down_mine)
    down = jnp.concatenate([down_mine, down_theirs], axis=0)

    partial = (dot_nt(hidden[quarter:], down) * PARTIAL_STEP).astype(f16)
    arrived = [
        shifted(partial[(k - 1) * quarter : k * quarter], "grp", GRP, k) for k in range(1, GRP)
    ]
    mixed = jnp.concatenate([states_mine[:quarter], states_theirs[:quarter]], axis=1).astype(f32)
    mixed = mixed + dot_nt(hidden[:quarter], down)
    for piece in arrived:
        mixed = mixed + piece.astype(f32) * (1.0 / PARTIAL_STEP)
    centred = mixed - jnp.mean(mixed, axis=-1, keepdims=True)
    inverse = lax.rsqrt(jnp.mean(centred * centred, axis=-1, keepdims=True) + 1e-05)
    normed = centred * inverse
    table = segment_table(query_lengths[0], passage_lengths[0], tokens, member * quarter)
    pooled = sum_permutes(dot_tn(table[:quarter], normed, EXACT), "grp", GRP) * gain_local
    scale = lax.rsqrt(jnp.sum(pooled * pooled, axis=-1, keepdims=True) + 1e-06)
    embed = pooled * scale

    centred_sent = centred.astype(bf16)
    quarters = [centred_sent] + [shifted(centred_sent, "grp", GRP, GRP - k) for k in range(1, GRP)]
    slope = gelu_slope(upward)

    listed = jnp.concatenate([positive[:, None], negatives], axis=1)
    owner = listed // queries
    listed = ((owner % CORE) * (Y * Z) + owner // CORE) * queries + listed % queries
    lanes = jnp.pad(listed.astype(f32), ((0, queries), (0, 128 - listed.shape[1])))
    sent = jnp.concatenate([swap_halves(embed) * EMBED_STEP, lanes], axis=1).astype(f16)
    mine = spread(sent, "z", Z)
    mine, slope = lax.optimization_barrier((mine, slope))
    mine = spread(mine, "y", Y)
    theirs = other_core(mine)
    first = jnp.where(core == 0, mine, theirs).astype(f32).reshape(Y * Z, 2 * queries, width + 128)
    second = jnp.where(core == 0, theirs, mine).astype(f32).reshape(Y * Z, 2 * queries, width + 128)
    d_logits, loss, d_sums = all_losses(
        jnp.stack([core, block]).astype(jnp.int32), first, second, embed, scale, gain_local,
        listed.shape[1],
    )
    d_mine, d_theirs, mine_turned, theirs_turned = norm_back(d_sums, table, quarters)

    d_sent = other_core(theirs_turned)
    d_upward = pair_call(slope_kernel, (d_mine, down_mine, d_theirs, down_theirs, slope), hidden.shape)
    d_upward_sent = other_core(d_upward)
    down_half = pair_call(
        down_kernel, (mine_turned, hidden, d_sent, hidden_sent), (half, hidden.shape[1])
    )
    pieces = pair_call(
        both_kernel,
        (states_mine, d_upward, states_sent, d_upward_sent, down_half),
        (Y, 2, half // Y, hidden.shape[1]),
    )
    sums = jnp.sum(lax.all_to_all(pieces, "y", 0, 0).astype(f32), axis=0)
    last = jnp.concatenate(
        [sums[0].reshape(Z, owned, -1), sums[1].reshape(Z, owned, -1)], axis=1
    )
    last = scatter_scaled(last, "z")
    grad_up = last[:owned]
    grad_down = last[owned:].T

    d_logits, first, second, _ = lax.optimization_barrier((d_logits, first, second, pieces))
    both = jnp.concatenate([first, second], axis=0)[:, :, :width]
    all_queries = both[:, :queries].reshape(-1, width) * (1.0 / EMBED_STEP)
    all_passages = both[:, queries:].reshape(-1, width) * (1.0 / EMBED_STEP)
    drawn = jnp.dot(d_logits, all_queries, precision=THREE)
    product = drawn * all_passages
    from_passages = jnp.sum(product, axis=1, keepdims=True)
    from_queries = jnp.sum(
        dot_tn(d_logits, all_passages, THREE) * all_queries, axis=1, keepdims=True
    )
    grad_gain = (
        2.0 * jnp.sum(product, axis=0)
        - jnp.sum(from_queries * all_queries * all_queries, axis=0)
        - jnp.sum(from_passages * all_passages * all_passages, axis=0)
    ) / TEMPER / gain_common[0]
    grad_gain = grad_gain.reshape(CORE, Y * Z, owned).transpose(1, 0, 2).reshape(width)
    return (loss[0, 0], grad_up, grad_down, grad_gain)


def solution(mesh):
    split = Mesh(mesh.devices.reshape(Y, Z, CORE, GRP), ("y", "z", "core", "grp"))
    dp = ("y", "z", "core")
    return jax.shard_map(
        shards,
        mesh=split,
        in_specs=(
            P(dp, None),
            P(dp, "grp"),
            P("grp", dp),
            P(),
            P(dp, None),
            P(dp, None),
            P(dp),
            P(dp, None),
        ),
        out_specs=(P(), P(dp, "grp"), P("grp", dp), P()),
        check_vma=False,
    )
```

```python
import functools

import jax
import jax.numpy as jnp
from jax import lax
from jax.experimental import pallas as pl
from jax.experimental.pallas import tpu as pltpu
from jax.sharding import Mesh, PartitionSpec as P

QTOK = 128
Y, Z, CORE, GRP = 4, 8, 2, 4
TEMPER = 0.02
EMBED_STEP = 1024.0
PARTIAL_STEP = 0.25
f32, bf16, f16 = jnp.float32, jnp.bfloat16, jnp.float16
EXACT = lax.Precision.HIGHEST
THREE = lax.Precision.HIGH


def normal_cdf(values):
    return 0.5 * (1.0 + lax.erf(values * 0.7071067811865476))


def gelu_exact(values):
    return values * normal_cdf(values)


def gelu_slope(values):
    return normal_cdf(values) + values * jnp.exp(-0.5 * values * values) * 0.3989422804014327


def segment_table(query_lengths, passage_lengths, total, shift):
    query_starts = jnp.cumsum(query_lengths) - query_lengths
    passage_starts = QTOK + jnp.cumsum(passage_lengths) - passage_lengths
    starts = jnp.concatenate([query_starts, passage_starts])
    lengths = jnp.concatenate([query_lengths, passage_lengths])
    places = ((jnp.arange(total, dtype=jnp.int32) + shift) % total)[:, None]
    inside = (places >= starts[None, :]) & (places < (starts + lengths)[None, :])
    return inside.astype(f32) / lengths.astype(f32)[None, :]


def spread(value, axis, count):
    return lax.all_to_all(jnp.broadcast_to(value[None], (count,) + value.shape), axis, 0, 0)


def other_core(value):
    return lax.ppermute(value, "core", [(0, 1), (1, 0)])


def shifted(value, axis, count, step):
    return lax.ppermute(value, axis, [(j, (j + step) % count) for j in range(count)])


def send_shifted(value, axis, count):
    return [shifted(value, axis, count, k) for k in range(1, count)]


def place_kernel(place, *refs):
    *pieces, out = refs
    count = len(pieces)
    for k, piece in enumerate(pieces):
        out[lax.rem(place[0] + count - k, count)] = piece[...]


def place_pieces(value, moved, axis):
    pieces = [value, *moved]
    vmem = pl.BlockSpec(memory_space=pltpu.VMEM)
    return pl.pallas_call(
        place_kernel,
        out_shape=jax.ShapeDtypeStruct((len(pieces),) + value.shape, value.dtype),
        in_specs=[pl.BlockSpec(memory_space=pltpu.SMEM)] + [vmem] * len(pieces),
        out_specs=vmem,
        compiler_params=pltpu.CompilerParams(vmem_limit_bytes=6 * 1024 * 1024),
        cost_estimate=pl.CostEstimate(flops=0, bytes_accessed=2**21, transcendentals=0),
    )(lax.axis_index(axis).reshape(1).astype(jnp.int32), *pieces)


def sum_permutes(value, axis, count):
    place = lax.axis_index(axis)
    moved = jnp.stack([value] + [shifted(value, axis, count, k) for k in range(1, count)])
    total = lax.dynamic_index_in_dim(moved, place, 0, keepdims=False)
    for k in range(1, count):
        total = total + lax.dynamic_index_in_dim(moved, (place - k) % count, 0, keepdims=False)
    return total


def dot_nt(a, b, precision=None):
    return lax.dot_general(
        a, b, (((1,), (1,)), ((), ())), precision=precision, preferred_element_type=f32
    )


def dot_tn(a, b, precision=None):
    return lax.dot_general(
        a, b, (((0,), (0,)), ((), ())), precision=precision, preferred_element_type=f32
    )


def split_high(value):
    high = value.astype(bf16)
    return high, (value - high.astype(f32)).astype(bf16)


def three_nn(a, high, low):
    a_high, a_low = split_high(a)
    dot = functools.partial(jnp.dot, preferred_element_type=f32)
    return dot(a_high, high[...]) + (dot(a_high, low[...]) + dot(a_low, high[...]))


def loss_kernel(
    scalars, first, second, embed, scale, gain,
    d_logits, loss, d_sums, q_high, q_low, p_high, p_low, logits, times, ids,
):
    core, block = scalars[0], scalars[1]
    half_count = first.shape[0] * 8
    count, width = q_high.shape
    half = width // 2
    listed = ids.shape[0]

    def split(i, carry):
        for source, base in ((first, 0), (second, half_count)):
            rows = pl.ds(pl.multiple_of(base + 16 * i, 16), 16)
            for offset, high, low in ((0, q_high, q_low), (8, p_high, p_low)):
                value = source[pl.ds(2 * i, 2), offset : offset + 8, :width].reshape(16, width)
                high[rows, :], low[rows, :] = split_high(value)
        return carry

    lax.fori_loop(0, half_count // 16, split, 0)
    lanes = [source[:, 0:8, width:].reshape(half_count, 128) for source in (first, second)]
    ids[...] = jnp.concatenate(lanes, axis=0).T[:listed]

    to_logits = 1.0 / (TEMPER * EMBED_STEP * EMBED_STEP)
    raw = dot_nt(p_high[...], q_high[...])
    raw = raw + (dot_nt(p_high[...], q_low[...]) + dot_nt(p_low[...], q_high[...]))
    logits[...] = raw * to_logits

    step = 32
    columns = lax.broadcasted_iota(jnp.int32, (step, count), 1) >> 3
    offsets = lax.broadcasted_iota(jnp.int32, (step, count), 0)

    def fold(value):
        return value.reshape(step // 8, 8, count)

    def count_times(i, carry):
        top, named = carry
        rows = pl.ds(pl.multiple_of(i * step, step), step)
        places = offsets + i * step
        whole = places.astype(f32)
        is_first = whole == ids[0:1, :]
        total = jnp.where(is_first, 1.0, 0.0) + jnp.where((places >> 3) == columns, 1.0, 0.0)
        for k in range(1, listed):
            total = total + jnp.where(whole == ids[k : k + 1, :], 1.0, 0.0)
        value = logits[rows, :]
        times[rows, :] = total
        top = jnp.maximum(top, jnp.max(fold(jnp.where(total > 0.0, value, -1e30)), axis=0))
        return top, named + jnp.sum(fold(jnp.where(is_first, value, 0.0)), axis=0)

    start = (jnp.full((8, count), -1e30, f32), jnp.zeros((8, count), f32))
    top, named = lax.fori_loop(0, count // step, count_times, start)
    top = jnp.max(top, axis=0, keepdims=True)
    named = jnp.sum(named, axis=0, keepdims=True)

    def weigh(i, carry):
        rows = pl.ds(pl.multiple_of(i * step, step), step)
        total = times[rows, :]
        weight = total * jnp.exp(jnp.where(total > 0.0, logits[rows, :] - top, 0.0))
        times[rows, :] = weight
        return carry + jnp.sum(fold(weight), axis=0)

    total = lax.fori_loop(0, count // step, weigh, jnp.zeros((8, count), f32))
    total = jnp.sum(total, axis=0, keepdims=True)
    loss[...] = jnp.broadcast_to(
        jnp.sum(jnp.log(total) + top - named, axis=1, keepdims=True) / count, loss.shape
    )
    share = 1.0 / total

    def differ(i, carry):
        rows = pl.ds(pl.multiple_of(i * step, step), step)
        is_first = (offsets + i * step).astype(f32) == ids[0:1, :]
        d_logits[rows, :] = times[rows, :] * share - jnp.where(is_first, 1.0, 0.0)
        return carry

    lax.fori_loop(0, count // step, differ, 0)

    own_place = block * 8
    picks = lax.broadcasted_iota(jnp.int32, (16, count), 0)
    picks = (lax.broadcasted_iota(jnp.int32, (16, count), 1) == picks + own_place) & (picks < 8)
    picks = jnp.where(picks, 1.0, 0.0).astype(bf16)
    d_high, d_low = split_high(d_logits[...])
    own_queries = dot_nt(picks, d_high) + dot_nt(picks, d_low)
    own_passages = d_logits[pl.ds(pl.multiple_of(own_place, 8), 8), :]
    own_passages = jnp.concatenate([own_passages, jnp.zeros_like(own_passages)], axis=0)
    d_embed = jnp.concatenate(
        [
            three_nn(own_queries, p_high, p_low)[:8],
            three_nn(own_passages, q_high, q_low)[:8],
        ],
        axis=0,
    ) * (1.0 / (TEMPER * EMBED_STEP))
    turned = jnp.concatenate([d_embed[:, half:], d_embed[:, :half]], axis=1)
    d_embed = jnp.where(core == 0, d_embed, turned)
    owned = embed[...]
    inner = jnp.sum(owned * d_embed, axis=1, keepdims=True)
    d_sums[...] = scale[...] * (d_embed - owned * inner) * gain[...]


def back_kernel(
    d_sums, table, own, next1, next2, next3, down_mine, down_theirs, slope,
    d_upward, mine_turned, theirs_turned,
):
    half = mine_turned.shape[0]
    value_high, value_low = split_high(d_sums[...])
    dot = functools.partial(jnp.dot, preferred_element_type=f32)
    for k, source in enumerate((own, next1, next2, next3)):
        size = source.shape[0]
        places = slice(k * size, (k + 1) * size)
        centred = source[...].astype(f32)
        inverse = lax.rsqrt(jnp.mean(centred * centred, axis=1, keepdims=True) + 1e-05)
        normed = centred * inverse
        part_high, part_low = split_high(table[places, :])
        d_normed = dot(part_high, value_high) + (
            dot(part_high, value_low) + dot(part_low, value_high)
        )
        d_mixed = inverse * (
            d_normed
            - jnp.mean(d_normed, axis=1, keepdims=True)
            - normed * jnp.mean(d_normed * normed, axis=1, keepdims=True)
        )
        d_hidden = dot(d_mixed[:, :half].astype(bf16), down_mine[...])
        d_hidden = d_hidden + dot(d_mixed[:, half:].astype(bf16), down_theirs[...])
        d_upward[places, :] = (d_hidden * slope[places, :]).astype(bf16)
        mine_turned[:, places] = d_mixed[:, :half].T.astype(bf16)
        theirs_turned[:, places] = d_mixed[:, half:].T.astype(bf16)


def own_kernel(a, b, c, d, up, down):
    step = 128
    for row in range(0, up.shape[0], step):
        rows = slice(row, row + step)
        up[rows, :] = dot_tn(a[:, rows], b[...])
        down[rows, :] = jnp.dot(c[rows, :], d[...], preferred_element_type=f32)


def other_kernel(place, up, down, a, b, c, d, own, next1, next2, next3, along_z):
    step = own.shape[1]
    split = own.shape[2]
    owned = along_z.shape[3]
    for k, out in enumerate((own, next1, next2, next3)):
        member = lax.rem(place[0] + k, Y)
        rows = pl.ds(pl.multiple_of(member * step, step), step)
        totals = (
            up[rows, :] + dot_tn(a[:, rows], b[...]),
            down[rows, :] + jnp.dot(c[rows, :], d[...], preferred_element_type=f32),
        )
        for part, total in enumerate(totals):
            out[part] = total[:, :split].astype(out.dtype)
            rest = total[:, split:].astype(bf16)
            for z in range(Z):
                along_z[z, part, member] = rest[z * owned : (z + 1) * owned]


def own_gradients(states, d_upward, d_turned, hidden):
    vmem = pl.BlockSpec(memory_space=pltpu.VMEM)
    shape = jax.ShapeDtypeStruct((d_turned.shape[0], hidden.shape[1]), f32)
    return pl.pallas_call(
        own_kernel,
        out_shape=(shape, shape),
        in_specs=[vmem] * 4,
        out_specs=(vmem, vmem),
        compiler_params=pltpu.CompilerParams(vmem_limit_bytes=12 * 1024 * 1024),
        cost_estimate=pl.CostEstimate(flops=2**31, bytes_accessed=2**16, transcendentals=0),
    )(states, d_upward, d_turned, hidden)


def all_gradients(up, down, states, d_upward, d_turned, hidden, owned):
    step, columns = up.shape[0] // Y, up.shape[1]
    split = columns * 3 // 4
    vmem = pl.BlockSpec(memory_space=pltpu.VMEM)
    piece = (2, step, split)
    return pl.pallas_call(
        other_kernel,
        out_shape=(jax.ShapeDtypeStruct(piece, f32),)
        + (jax.ShapeDtypeStruct(piece, bf16),) * (Y - 1)
        + (jax.ShapeDtypeStruct((Z, 2, Y, owned, columns - split), bf16),),
        in_specs=[pl.BlockSpec(memory_space=pltpu.SMEM)] + [vmem] * 6,
        out_specs=(vmem,) * (Y + 1),
        compiler_params=pltpu.CompilerParams(vmem_limit_bytes=16 * 1024 * 1024),
        cost_estimate=pl.CostEstimate(flops=2**31, bytes_accessed=2**22, transcendentals=0),
    )(
        lax.axis_index("y").reshape(1).astype(jnp.int32),
        up, down, states, d_upward, d_turned, hidden,
    )


def scale_kernel(own, next1, next2, next3, out):
    owned = out.shape[1] // 2
    width = own.shape[2]
    for z in range(out.shape[0]):
        for part in range(2):
            rows = slice(z * owned, (z + 1) * owned)
            total = own[part, rows, :]
            for piece in (next1, next2, next3):
                total = total + piece[part, rows, :].astype(f32)
            largest = jnp.max(jnp.abs(total), axis=1, keepdims=True)
            exponent = jnp.floor(jnp.log(jnp.maximum(largest, 1e-30)) * 1.4426950408889634)
            places = slice(part * owned, (part + 1) * owned)
            out[z, places, :width] = total * jnp.exp(exponent * -0.6931471805599453)
            out[z, places, width:] = jnp.broadcast_to(exponent, (owned, 128))


def scale_rows(own, moved):
    parts, rows, columns = own.shape
    vmem = pl.BlockSpec(memory_space=pltpu.VMEM)
    return pl.pallas_call(
        scale_kernel,
        out_shape=jax.ShapeDtypeStruct((Z, parts * rows // Z, columns + 128), f32),
        in_specs=[vmem] * (1 + len(moved)),
        out_specs=vmem,
        compiler_params=pltpu.CompilerParams(vmem_limit_bytes=8 * 1024 * 1024),
        cost_estimate=pl.CostEstimate(flops=2**20, bytes_accessed=2**22, transcendentals=0),
    )(own, *moved)


def all_losses(scalars, first, second, embed, scale, gain, listed):
    count, width = first.shape[0] * 16, embed.shape[1]
    vmem = pl.BlockSpec(memory_space=pltpu.VMEM)
    return pl.pallas_call(
        loss_kernel,
        out_shape=(
            jax.ShapeDtypeStruct((count, count), f32),
            jax.ShapeDtypeStruct((8, 128), f32),
            jax.ShapeDtypeStruct(embed.shape, f32),
        ),
        in_specs=[pl.BlockSpec(memory_space=pltpu.SMEM)] + [vmem] * 5,
        out_specs=(vmem,) * 3,
        scratch_shapes=[pltpu.VMEM((count, width), bf16)] * 4
        + [pltpu.VMEM((count, count), f32)] * 2
        + [pltpu.VMEM((listed, count), f32)],
        compiler_params=pltpu.CompilerParams(vmem_limit_bytes=22 * 1024 * 1024),
        cost_estimate=pl.CostEstimate(flops=2**20, bytes_accessed=2**16, transcendentals=0),
    )(scalars, first, second, embed, scale, gain)


def norm_back(d_sums, table, quarters, down_mine, down_theirs, slope):
    tokens, half = table.shape[0], d_sums.shape[1] // 2
    vmem = pl.BlockSpec(memory_space=pltpu.VMEM)
    return pl.pallas_call(
        back_kernel,
        out_shape=(jax.ShapeDtypeStruct(slope.shape, bf16),)
        + (jax.ShapeDtypeStruct((half, tokens), bf16),) * 2,
        in_specs=[vmem] * (5 + len(quarters)),
        out_specs=(vmem,) * 3,
        compiler_params=pltpu.CompilerParams(vmem_limit_bytes=14 * 1024 * 1024),
        cost_estimate=pl.CostEstimate(flops=2**20, bytes_accessed=2**16, transcendentals=0),
    )(d_sums, table, *quarters, down_mine, down_theirs, slope)


def shards(states, w_up, w_down, gain, query_lengths, passage_lengths, positive, negatives):
    tokens, width = states.shape
    half = width // 2
    owned = w_up.shape[0]
    quarter = tokens // GRP
    queries = positive.shape[0]
    core = lax.axis_index("core")
    member = lax.axis_index("grp")
    block = core * (Y * Z) + lax.axis_index("y") * Z + lax.axis_index("z")

    def swap_halves(value):
        return jnp.where(core == 0, value, jnp.roll(value, half, axis=-1))

    def turn(value):
        parts = value.reshape((GRP, quarter) + value.shape[1:])
        order = [lax.dynamic_index_in_dim(parts, (member + k) % GRP, 0, keepdims=False) for k in range(GRP)]
        return jnp.concatenate(order, axis=0)

    cores = turn(states).reshape(tokens, Y * Z, CORE, owned).transpose(2, 0, 1, 3).reshape(CORE, tokens, half)
    states_mine = lax.dynamic_index_in_dim(cores, core, 0, keepdims=False)
    states_theirs = lax.dynamic_index_in_dim(cores, 1 - core, 0, keepdims=False)
    gain_common = gain.reshape(Y * Z, CORE, owned).transpose(1, 0, 2).reshape(1, width)
    gain_local = swap_halves(gain_common)

    up_z = spread(w_up, "z", Z)
    up_z, states_mine, states_theirs, down_sent = lax.optimization_barrier(
        (up_z, states_mine, states_theirs, w_down.T)
    )
    down_z = spread(down_sent, "z", Z)
    up_moved = send_shifted(up_z, "y", Y)
    up_moved, down_z = lax.optimization_barrier((up_moved, down_z))
    up_mine = place_pieces(up_z, up_moved, "y").reshape(half, -1)
    up_theirs = other_core(up_mine)
    down_moved = send_shifted(down_z, "y", Y)
    states_sent = other_core(states_theirs)

    upward = jnp.dot(states_mine, up_mine, preferred_element_type=f32) + jnp.dot(
        states_theirs, up_theirs, preferred_element_type=f32
    )
    hidden = gelu_exact(upward).astype(bf16)
    hidden, down_moved = lax.optimization_barrier((hidden, down_moved))
    hidden_sent = other_core(hidden)
    down_mine = place_pieces(down_z, down_moved, "y").reshape(half, -1)
    down_theirs = other_core(down_mine)
    down = jnp.concatenate([down_mine, down_theirs], axis=0)

    partial = (dot_nt(hidden[quarter:], down) * PARTIAL_STEP).astype(f16)
    arrived = [
        shifted(partial[(k - 1) * quarter : k * quarter], "grp", GRP, k) for k in range(1, GRP)
    ]
    mixed = jnp.concatenate([states_mine[:quarter], states_theirs[:quarter]], axis=1).astype(f32)
    mixed = mixed + dot_nt(hidden[:quarter], down)
    for piece in arrived:
        mixed = mixed + piece.astype(f32) * (1.0 / PARTIAL_STEP)
    centred = mixed - jnp.mean(mixed, axis=-1, keepdims=True)
    inverse = lax.rsqrt(jnp.mean(centred * centred, axis=-1, keepdims=True) + 1e-05)
    normed = centred * inverse
    table = segment_table(query_lengths[0], passage_lengths[0], tokens, member * quarter)
    pooled = sum_permutes(dot_tn(table[:quarter], normed, EXACT), "grp", GRP) * gain_local
    scale = lax.rsqrt(jnp.sum(pooled * pooled, axis=-1, keepdims=True) + 1e-06)
    embed = pooled * scale

    centred_sent = centred.astype(bf16)
    quarters = [centred_sent] + [shifted(centred_sent, "grp", GRP, GRP - k) for k in range(1, GRP)]
    slope = gelu_slope(upward)

    listed = jnp.concatenate([positive[:, None], negatives], axis=1)
    owner = listed // queries
    listed = ((owner % CORE) * (Y * Z) + owner // CORE) * queries + listed % queries
    lanes = jnp.pad(listed.astype(f32), ((0, queries), (0, 128 - listed.shape[1])))
    sent = jnp.concatenate([swap_halves(embed) * EMBED_STEP, lanes], axis=1).astype(f16)
    mine = spread(sent, "z", Z)
    mine, slope = lax.optimization_barrier((mine, slope))
    mine = spread(mine, "y", Y)
    mine, *quarters = lax.optimization_barrier((mine, *quarters))
    theirs = other_core(mine)
    first = jnp.where(core == 0, mine, theirs).astype(f32).reshape(Y * Z, 2 * queries, width + 128)
    second = jnp.where(core == 0, theirs, mine).astype(f32).reshape(Y * Z, 2 * queries, width + 128)
    d_logits, loss, d_sums = all_losses(
        jnp.stack([core, block]).astype(jnp.int32), first, second, embed, scale, gain_local,
        listed.shape[1],
    )
    d_upward, mine_turned, theirs_turned = norm_back(
        d_sums, table, quarters, down_mine, down_theirs, slope
    )

    d_sent = other_core(theirs_turned)
    d_upward_sent = other_core(d_upward)
    up_own, down_own = own_gradients(states_mine, d_upward, mine_turned, hidden)
    own, *pieces, along_z = all_gradients(
        up_own, down_own, states_sent, d_upward_sent, d_sent, hidden_sent, owned
    )
    moved = [shifted(piece, "y", Y, k) for k, piece in enumerate(pieces, 1)]
    arrived = lax.all_to_all(along_z, "z", 0, 0)
    split = own.shape[2]
    scaled = lax.all_to_all(scale_rows(own, moved).astype(f16), "z", 0, 0)
    factor = jnp.exp2(scaled[..., split : split + 1].astype(f32))
    large = jnp.sum(scaled[..., :split].astype(f32) * factor, axis=0).reshape(2, owned, split)
    sums = jnp.sum(arrived.astype(f32), axis=0)
    place = lax.axis_index("y")
    small = lax.dynamic_index_in_dim(sums, place, 1, keepdims=False)
    for k in range(1, Y):
        piece = lax.dynamic_index_in_dim(sums, (place + k) % Y, 1, keepdims=False)
        small = small + shifted(piece, "y", Y, k)
    both = jnp.concatenate([large, small], axis=-1)
    grad_up = both[0]
    grad_down = both[1].T

    d_logits, first, second, _ = lax.optimization_barrier((d_logits, first, second, own))
    both = jnp.concatenate([first, second], axis=0)[:, :, :width]
    all_queries = both[:, :queries].reshape(-1, width) * (1.0 / EMBED_STEP)
    all_passages = both[:, queries:].reshape(-1, width) * (1.0 / EMBED_STEP)
    drawn = jnp.dot(d_logits, all_queries, precision=THREE)
    product = drawn * all_passages
    from_passages = jnp.sum(product, axis=1, keepdims=True)
    from_queries = jnp.sum(
        dot_tn(d_logits, all_passages, THREE) * all_queries, axis=1, keepdims=True
    )
    grad_gain = (
        2.0 * jnp.sum(product, axis=0)
        - jnp.sum(from_queries * all_queries * all_queries, axis=0)
        - jnp.sum(from_passages * all_passages * all_passages, axis=0)
    ) / TEMPER / gain_common[0]
    grad_gain = grad_gain.reshape(CORE, Y * Z, owned).transpose(1, 0, 2).reshape(width)
    return (loss[0, 0], grad_up, grad_down, grad_gain)


def solution(mesh):
    split = Mesh(mesh.devices.reshape(Y, Z, CORE, GRP), ("y", "z", "core", "grp"))
    dp = ("y", "z", "core")
    return jax.shard_map(
        shards,
        mesh=split,
        in_specs=(
            P(dp, None),
            P(dp, "grp"),
            P("grp", dp),
            P(),
            P(dp, None),
            P(dp, None),
            P(dp),
            P(dp, None),
        ),
        out_specs=(P(), P(dp, "grp"), P("grp", dp), P()),
        check_vma=False,
    )
```

```python
import functools

import jax
import jax.numpy as jnp
from jax import lax
from jax.experimental import pallas as pl
from jax.experimental.pallas import tpu as pltpu
from jax.sharding import Mesh, PartitionSpec as P

QTOK = 128
Y, Z, CORE, GRP = 4, 8, 2, 4
TEMPER = 0.02
EMBED_STEP = 1024.0
PARTIAL_STEP = 0.25
f32, bf16, f16 = jnp.float32, jnp.bfloat16, jnp.float16
EXACT = lax.Precision.HIGHEST
THREE = lax.Precision.HIGH


def normal_cdf(values):
    return 0.5 * (1.0 + lax.erf(values * 0.7071067811865476))


def gelu_exact(values):
    return values * normal_cdf(values)


def gelu_slope(values):
    return normal_cdf(values) + values * jnp.exp(-0.5 * values * values) * 0.3989422804014327


def segment_table(query_lengths, passage_lengths, total, shift):
    query_starts = jnp.cumsum(query_lengths) - query_lengths
    passage_starts = QTOK + jnp.cumsum(passage_lengths) - passage_lengths
    starts = jnp.concatenate([query_starts, passage_starts])
    lengths = jnp.concatenate([query_lengths, passage_lengths])
    places = ((jnp.arange(total, dtype=jnp.int32) + shift) % total)[:, None]
    inside = (places >= starts[None, :]) & (places < (starts + lengths)[None, :])
    return inside.astype(f32) / lengths.astype(f32)[None, :]


def spread(value, axis, count):
    return lax.all_to_all(jnp.broadcast_to(value[None], (count,) + value.shape), axis, 0, 0)


def other_core(value):
    return lax.ppermute(value, "core", [(0, 1), (1, 0)])


def shifted(value, axis, count, step):
    return lax.ppermute(value, axis, [(j, (j + step) % count) for j in range(count)])


def send_shifted(value, axis, count):
    return [shifted(value, axis, count, k) for k in range(1, count)]


def place_kernel(place, *refs):
    *pieces, out = refs
    count = len(pieces)
    for k, piece in enumerate(pieces):
        out[lax.rem(place[0] + count - k, count)] = piece[...]


def place_pieces(value, moved, axis):
    pieces = [value, *moved]
    vmem = pl.BlockSpec(memory_space=pltpu.VMEM)
    return pl.pallas_call(
        place_kernel,
        out_shape=jax.ShapeDtypeStruct((len(pieces),) + value.shape, value.dtype),
        in_specs=[pl.BlockSpec(memory_space=pltpu.SMEM)] + [vmem] * len(pieces),
        out_specs=vmem,
        compiler_params=pltpu.CompilerParams(vmem_limit_bytes=16 * 1024 * 1024),
        cost_estimate=pl.CostEstimate(flops=0, bytes_accessed=2**21, transcendentals=0),
    )(lax.axis_index(axis).reshape(1).astype(jnp.int32), *pieces)


def sum_permutes(value, axis, count):
    place = lax.axis_index(axis)
    moved = jnp.stack([value] + [shifted(value, axis, count, k) for k in range(1, count)])
    total = lax.dynamic_index_in_dim(moved, place, 0, keepdims=False)
    for k in range(1, count):
        total = total + lax.dynamic_index_in_dim(moved, (place - k) % count, 0, keepdims=False)
    return total


def dot_nt(a, b, precision=None):
    return lax.dot_general(
        a, b, (((1,), (1,)), ((), ())), precision=precision, preferred_element_type=f32
    )


def dot_tn(a, b, precision=None):
    return lax.dot_general(
        a, b, (((0,), (0,)), ((), ())), precision=precision, preferred_element_type=f32
    )


def split_high(value):
    high = value.astype(bf16)
    return high, (value - high.astype(f32)).astype(bf16)


def three_nn(a, high, low):
    a_high, a_low = split_high(a)
    dot = functools.partial(jnp.dot, preferred_element_type=f32)
    return dot(a_high, high[...]) + (dot(a_high, low[...]) + dot(a_low, high[...]))


def loss_kernel(
    scalars, first, second, embed, scale, gain,
    d_logits, loss, d_sums, q_high, q_low, p_high, p_low, logits, times, ids,
):
    core, block = scalars[0], scalars[1]
    half_count = first.shape[0] * 8
    count, width = q_high.shape
    half = width // 2
    listed = ids.shape[0]

    def split(i, carry):
        for source, base in ((first, 0), (second, half_count)):
            rows = pl.ds(pl.multiple_of(base + 16 * i, 16), 16)
            for offset, high, low in ((0, q_high, q_low), (8, p_high, p_low)):
                value = source[pl.ds(2 * i, 2), offset : offset + 8, :width].reshape(16, width)
                high[rows, :], low[rows, :] = split_high(value)
        return carry

    lax.fori_loop(0, half_count // 16, split, 0)
    lanes = [source[:, 0:8, width:].reshape(half_count, 128) for source in (first, second)]
    ids[...] = jnp.concatenate(lanes, axis=0).T[:listed]

    to_logits = 1.0 / (TEMPER * EMBED_STEP * EMBED_STEP)
    raw = dot_nt(p_high[...], q_high[...])
    raw = raw + (dot_nt(p_high[...], q_low[...]) + dot_nt(p_low[...], q_high[...]))
    logits[...] = raw * to_logits

    step = 32
    columns = lax.broadcasted_iota(jnp.int32, (step, count), 1) >> 3
    offsets = lax.broadcasted_iota(jnp.int32, (step, count), 0)

    def fold(value):
        return value.reshape(step // 8, 8, count)

    def count_times(i, carry):
        top, named = carry
        rows = pl.ds(pl.multiple_of(i * step, step), step)
        places = offsets + i * step
        whole = places.astype(f32)
        is_first = whole == ids[0:1, :]
        total = jnp.where(is_first, 1.0, 0.0) + jnp.where((places >> 3) == columns, 1.0, 0.0)
        for k in range(1, listed):
            total = total + jnp.where(whole == ids[k : k + 1, :], 1.0, 0.0)
        value = logits[rows, :]
        times[rows, :] = total
        top = jnp.maximum(top, jnp.max(fold(jnp.where(total > 0.0, value, -1e30)), axis=0))
        return top, named + jnp.sum(fold(jnp.where(is_first, value, 0.0)), axis=0)

    start = (jnp.full((8, count), -1e30, f32), jnp.zeros((8, count), f32))
    top, named = lax.fori_loop(0, count // step, count_times, start)
    top = jnp.max(top, axis=0, keepdims=True)
    named = jnp.sum(named, axis=0, keepdims=True)

    def weigh(i, carry):
        rows = pl.ds(pl.multiple_of(i * step, step), step)
        total = times[rows, :]
        weight = total * jnp.exp(jnp.where(total > 0.0, logits[rows, :] - top, 0.0))
        times[rows, :] = weight
        return carry + jnp.sum(fold(weight), axis=0)

    total = lax.fori_loop(0, count // step, weigh, jnp.zeros((8, count), f32))
    total = jnp.sum(total, axis=0, keepdims=True)
    loss[...] = jnp.broadcast_to(
        jnp.sum(jnp.log(total) + top - named, axis=1, keepdims=True) / count, loss.shape
    )
    share = 1.0 / total

    def differ(i, carry):
        rows = pl.ds(pl.multiple_of(i * step, step), step)
        is_first = (offsets + i * step).astype(f32) == ids[0:1, :]
        d_logits[rows, :] = times[rows, :] * share - jnp.where(is_first, 1.0, 0.0)
        return carry

    lax.fori_loop(0, count // step, differ, 0)

    own_place = block * 8
    picks = lax.broadcasted_iota(jnp.int32, (16, count), 0)
    picks = (lax.broadcasted_iota(jnp.int32, (16, count), 1) == picks + own_place) & (picks < 8)
    picks = jnp.where(picks, 1.0, 0.0).astype(bf16)
    d_high, d_low = split_high(d_logits[...])
    own_queries = dot_nt(picks, d_high) + dot_nt(picks, d_low)
    own_passages = d_logits[pl.ds(pl.multiple_of(own_place, 8), 8), :]
    own_passages = jnp.concatenate([own_passages, jnp.zeros_like(own_passages)], axis=0)
    d_embed = jnp.concatenate(
        [
            three_nn(own_queries, p_high, p_low)[:8],
            three_nn(own_passages, q_high, q_low)[:8],
        ],
        axis=0,
    ) * (1.0 / (TEMPER * EMBED_STEP))
    turned = jnp.concatenate([d_embed[:, half:], d_embed[:, :half]], axis=1)
    d_embed = jnp.where(core == 0, d_embed, turned)
    owned = embed[...]
    inner = jnp.sum(owned * d_embed, axis=1, keepdims=True)
    d_sums[...] = scale[...] * (d_embed - owned * inner) * gain[...]


def back_kernel(
    d_sums, table, own, next1, next2, next3, down_mine, down_theirs, slope,
    d_upward, mine_turned, theirs_turned,
):
    half = mine_turned.shape[0]
    value_high, value_low = split_high(d_sums[...])
    dot = functools.partial(jnp.dot, preferred_element_type=f32)
    for k, source in enumerate((own, next1, next2, next3)):
        size = source.shape[0]
        places = slice(k * size, (k + 1) * size)
        centred = source[...].astype(f32)
        inverse = lax.rsqrt(jnp.mean(centred * centred, axis=1, keepdims=True) + 1e-05)
        normed = centred * inverse
        part_high, part_low = split_high(table[places, :])
        d_normed = dot(part_high, value_high) + (
            dot(part_high, value_low) + dot(part_low, value_high)
        )
        d_mixed = inverse * (
            d_normed
            - jnp.mean(d_normed, axis=1, keepdims=True)
            - normed * jnp.mean(d_normed * normed, axis=1, keepdims=True)
        )
        d_hidden = dot(d_mixed[:, :half].astype(bf16), down_mine[...])
        d_hidden = d_hidden + dot(d_mixed[:, half:].astype(bf16), down_theirs[...])
        d_upward[places, :] = (d_hidden * slope[places, :]).astype(bf16)
        mine_turned[:, places] = d_mixed[:, :half].T.astype(bf16)
        theirs_turned[:, places] = d_mixed[:, half:].T.astype(bf16)


def own_kernel(a, b, c, d, up, down):
    step = 128
    for row in range(0, up.shape[0], step):
        rows = slice(row, row + step)
        up[rows, :] = dot_tn(a[:, rows], b[...])
        down[rows, :] = jnp.dot(c[rows, :], d[...], preferred_element_type=f32)


def other_kernel(up, down, a, b, c, d, out):
    out[0, 0] = (up[...] + dot_tn(a[...], b[...])).astype(bf16)
    out[0, 1] = (down[...] + jnp.dot(c[...], d[...], preferred_element_type=f32)).astype(bf16)


def own_gradients(states, d_upward, d_turned, hidden):
    vmem = pl.BlockSpec(memory_space=pltpu.VMEM)
    shape = jax.ShapeDtypeStruct((d_turned.shape[0], hidden.shape[1]), f32)
    return pl.pallas_call(
        own_kernel,
        out_shape=(shape, shape),
        in_specs=[vmem] * 4,
        out_specs=(vmem, vmem),
        compiler_params=pltpu.CompilerParams(vmem_limit_bytes=24 * 1024 * 1024),
        cost_estimate=pl.CostEstimate(flops=2**31, bytes_accessed=2**16, transcendentals=0),
    )(states, d_upward, d_turned, hidden)


def all_gradients(up, down, states, d_upward, d_turned, hidden):
    step, columns = up.shape[0] // Y, up.shape[1]
    vmem = pl.BlockSpec(memory_space=pltpu.VMEM)
    rows = pl.BlockSpec((step, columns), lambda k: (k, 0))
    return pl.pallas_call(
        other_kernel,
        grid=(Y,),
        out_shape=jax.ShapeDtypeStruct((Y, 2, step, columns), bf16),
        in_specs=[
            rows,
            rows,
            pl.BlockSpec((states.shape[0], step), lambda k: (0, k)),
            vmem,
            pl.BlockSpec((step, d_turned.shape[1]), lambda k: (k, 0)),
            vmem,
        ],
        out_specs=pl.BlockSpec((1, 2, step, columns), lambda k: (k, 0, 0, 0)),
        compiler_params=pltpu.CompilerParams(vmem_limit_bytes=24 * 1024 * 1024),
        cost_estimate=pl.CostEstimate(flops=2**31, bytes_accessed=2**22, transcendentals=0),
    )(up, down, states, d_upward, d_turned, hidden)


def scale_kernel(moved, out):
    owned = out.shape[1] // 2
    width = moved.shape[3]
    for z in range(out.shape[0]):
        for part in range(2):
            rows = slice(z * owned, (z + 1) * owned)
            total = moved[0, part, rows, :].astype(f32)
            for k in range(1, moved.shape[0]):
                total = total + moved[k, part, rows, :].astype(f32)
            largest = jnp.max(jnp.abs(total), axis=1, keepdims=True)
            exponent = jnp.floor(jnp.log(jnp.maximum(largest, 1e-30)) * 1.4426950408889634)
            places = slice(part * owned, (part + 1) * owned)
            out[z, places, :width] = total * jnp.exp(exponent * -0.6931471805599453)
            out[z, places, width:] = jnp.broadcast_to(exponent, (owned, 128))


def scale_rows(moved):
    count, parts, rows, columns = moved.shape
    vmem = pl.BlockSpec(memory_space=pltpu.VMEM)
    return pl.pallas_call(
        scale_kernel,
        out_shape=jax.ShapeDtypeStruct((Z, parts * rows // Z, columns + 128), f32),
        in_specs=[vmem],
        out_specs=vmem,
        compiler_params=pltpu.CompilerParams(vmem_limit_bytes=16 * 1024 * 1024),
        cost_estimate=pl.CostEstimate(flops=2**20, bytes_accessed=2**22, transcendentals=0),
    )(moved)


def all_losses(scalars, first, second, embed, scale, gain, listed):
    count, width = first.shape[0] * 16, embed.shape[1]
    vmem = pl.BlockSpec(memory_space=pltpu.VMEM)
    return pl.pallas_call(
        loss_kernel,
        out_shape=(
            jax.ShapeDtypeStruct((count, count), f32),
            jax.ShapeDtypeStruct((8, 128), f32),
            jax.ShapeDtypeStruct(embed.shape, f32),
        ),
        in_specs=[pl.BlockSpec(memory_space=pltpu.SMEM)] + [vmem] * 5,
        out_specs=(vmem,) * 3,
        scratch_shapes=[pltpu.VMEM((count, width), bf16)] * 4
        + [pltpu.VMEM((count, count), f32)] * 2
        + [pltpu.VMEM((listed, count), f32)],
        compiler_params=pltpu.CompilerParams(vmem_limit_bytes=40 * 1024 * 1024),
        cost_estimate=pl.CostEstimate(flops=2**20, bytes_accessed=2**16, transcendentals=0),
    )(scalars, first, second, embed, scale, gain)


def norm_back(d_sums, table, quarters, down_mine, down_theirs, slope):
    tokens, half = table.shape[0], d_sums.shape[1] // 2
    vmem = pl.BlockSpec(memory_space=pltpu.VMEM)
    return pl.pallas_call(
        back_kernel,
        out_shape=(jax.ShapeDtypeStruct(slope.shape, bf16),)
        + (jax.ShapeDtypeStruct((half, tokens), bf16),) * 2,
        in_specs=[vmem] * (5 + len(quarters)),
        out_specs=(vmem,) * 3,
        compiler_params=pltpu.CompilerParams(vmem_limit_bytes=24 * 1024 * 1024),
        cost_estimate=pl.CostEstimate(flops=2**20, bytes_accessed=2**16, transcendentals=0),
    )(d_sums, table, *quarters, down_mine, down_theirs, slope)


def shards(states, w_up, w_down, gain, query_lengths, passage_lengths, positive, negatives):
    tokens, width = states.shape
    half = width // 2
    owned = w_up.shape[0]
    quarter = tokens // GRP
    queries = positive.shape[0]
    core = lax.axis_index("core")
    member = lax.axis_index("grp")
    block = core * (Y * Z) + lax.axis_index("y") * Z + lax.axis_index("z")

    def swap_halves(value):
        return jnp.where(core == 0, value, jnp.roll(value, half, axis=-1))

    def turn(value):
        parts = value.reshape((GRP, quarter) + value.shape[1:])
        order = [lax.dynamic_index_in_dim(parts, (member + k) % GRP, 0, keepdims=False) for k in range(GRP)]
        return jnp.concatenate(order, axis=0)

    cores = turn(states).reshape(tokens, Y * Z, CORE, owned).transpose(2, 0, 1, 3).reshape(CORE, tokens, half)
    states_mine = lax.dynamic_index_in_dim(cores, core, 0, keepdims=False)
    states_theirs = lax.dynamic_index_in_dim(cores, 1 - core, 0, keepdims=False)
    gain_common = gain.reshape(Y * Z, CORE, owned).transpose(1, 0, 2).reshape(1, width)
    gain_local = swap_halves(gain_common)

    up_z = spread(w_up, "z", Z)
    up_z, states_mine, states_theirs, down_sent = lax.optimization_barrier(
        (up_z, states_mine, states_theirs, w_down.T)
    )
    down_z = spread(down_sent, "z", Z)
    up_moved = send_shifted(up_z, "y", Y)
    up_moved, down_z = lax.optimization_barrier((up_moved, down_z))
    up_mine = place_pieces(up_z, up_moved, "y").reshape(half, -1)
    up_theirs = other_core(up_mine)
    down_moved = send_shifted(down_z, "y", Y)
    states_sent = other_core(states_theirs)

    upward = jnp.dot(states_mine, up_mine, preferred_element_type=f32) + jnp.dot(
        states_theirs, up_theirs, preferred_element_type=f32
    )
    hidden = gelu_exact(upward).astype(bf16)
    hidden, down_moved = lax.optimization_barrier((hidden, down_moved))
    hidden_sent = other_core(hidden)
    down_mine = place_pieces(down_z, down_moved, "y").reshape(half, -1)
    down_theirs = other_core(down_mine)
    down = jnp.concatenate([down_mine, down_theirs], axis=0)

    partial = (dot_nt(hidden[quarter:], down) * PARTIAL_STEP).astype(f16)
    arrived = [
        shifted(partial[(k - 1) * quarter : k * quarter], "grp", GRP, k) for k in range(1, GRP)
    ]
    mixed = jnp.concatenate([states_mine[:quarter], states_theirs[:quarter]], axis=1).astype(f32)
    mixed = mixed + dot_nt(hidden[:quarter], down)
    for piece in arrived:
        mixed = mixed + piece.astype(f32) * (1.0 / PARTIAL_STEP)
    centred = mixed - jnp.mean(mixed, axis=-1, keepdims=True)
    inverse = lax.rsqrt(jnp.mean(centred * centred, axis=-1, keepdims=True) + 1e-05)
    normed = centred * inverse
    table = segment_table(query_lengths[0], passage_lengths[0], tokens, member * quarter)
    pooled = sum_permutes(dot_tn(table[:quarter], normed, EXACT), "grp", GRP) * gain_local
    scale = lax.rsqrt(jnp.sum(pooled * pooled, axis=-1, keepdims=True) + 1e-06)
    embed = pooled * scale

    centred_sent = centred.astype(bf16)
    quarters = [centred_sent] + [shifted(centred_sent, "grp", GRP, GRP - k) for k in range(1, GRP)]
    slope = gelu_slope(upward)

    listed = jnp.concatenate([positive[:, None], negatives], axis=1)
    owner = listed // queries
    listed = ((owner % CORE) * (Y * Z) + owner // CORE) * queries + listed % queries
    lanes = jnp.pad(listed.astype(f32), ((0, queries), (0, 128 - listed.shape[1])))
    sent = jnp.concatenate([swap_halves(embed) * EMBED_STEP, lanes], axis=1).astype(f16)
    mine = spread(sent, "z", Z)
    mine, slope = lax.optimization_barrier((mine, slope))
    mine = spread(mine, "y", Y)
    mine, *quarters = lax.optimization_barrier((mine, *quarters))
    theirs = other_core(mine)
    first = jnp.where(core == 0, mine, theirs).astype(f32).reshape(Y * Z, 2 * queries, width + 128)
    second = jnp.where(core == 0, theirs, mine).astype(f32).reshape(Y * Z, 2 * queries, width + 128)
    d_logits, loss, d_sums = all_losses(
        jnp.stack([core, block]).astype(jnp.int32), first, second, embed, scale, gain_local,
        listed.shape[1],
    )
    d_upward, mine_turned, theirs_turned = norm_back(
        d_sums, table, quarters, down_mine, down_theirs, slope
    )

    d_sent = other_core(theirs_turned)
    d_upward_sent = other_core(d_upward)
    up_own, down_own = own_gradients(states_mine, d_upward, mine_turned, hidden)
    pieces = all_gradients(up_own, down_own, states_sent, d_upward_sent, d_sent, hidden_sent)
    last = scale_rows(lax.all_to_all(pieces, "y", 0, 0)).astype(f16)
    last = lax.all_to_all(last, "z", 0, 0)
    factor = jnp.exp2(last[..., width : width + 1].astype(f32))
    last = jnp.sum(last[..., :width].astype(f32) * factor, axis=0)
    grad_up = last[:owned]
    grad_down = last[owned:].T

    d_logits, first, second, _ = lax.optimization_barrier((d_logits, first, second, pieces))
    both = jnp.concatenate([first, second], axis=0)[:, :, :width]
    all_queries = both[:, :queries].reshape(-1, width) * (1.0 / EMBED_STEP)
    all_passages = both[:, queries:].reshape(-1, width) * (1.0 / EMBED_STEP)
    drawn = jnp.dot(d_logits, all_queries, precision=THREE)
    product = drawn * all_passages
    from_passages = jnp.sum(product, axis=1, keepdims=True)
    from_queries = jnp.sum(
        dot_tn(d_logits, all_passages, THREE) * all_queries, axis=1, keepdims=True
    )
    grad_gain = (
        2.0 * jnp.sum(product, axis=0)
        - jnp.sum(from_queries * all_queries * all_queries, axis=0)
        - jnp.sum(from_passages * all_passages * all_passages, axis=0)
    ) / TEMPER / gain_common[0]
    grad_gain = grad_gain.reshape(CORE, Y * Z, owned).transpose(1, 0, 2).reshape(width)
    return (loss[0, 0], grad_up, grad_down, grad_gain)


def solution(mesh):
    split = Mesh(mesh.devices.reshape(Y, Z, CORE, GRP), ("y", "z", "core", "grp"))
    dp = ("y", "z", "core")
    return jax.shard_map(
        shards,
        mesh=split,
        in_specs=(
            P(dp, None),
            P(dp, "grp"),
            P("grp", dp),
            P(),
            P(dp, None),
            P(dp, None),
            P(dp),
            P(dp, None),
        ),
        out_specs=(P(), P(dp, "grp"), P("grp", dp), P()),
        check_vma=False,
    )
```

```python
import functools

import jax
import jax.numpy as jnp
from jax import lax
from jax.experimental import pallas as pl
from jax.experimental.pallas import tpu as pltpu
from jax.sharding import Mesh, PartitionSpec as P

QTOK = 128
Y, Z, CORE, GRP = 4, 8, 2, 4
TEMPER = 0.02
EMBED_STEP = 1024.0
PARTIAL_STEP = 0.25
f32, bf16, f16 = jnp.float32, jnp.bfloat16, jnp.float16
EXACT = lax.Precision.HIGHEST
THREE = lax.Precision.HIGH


def normal_cdf(values):
    return 0.5 * (1.0 + lax.erf(values * 0.7071067811865476))


def gelu_exact(values):
    return values * normal_cdf(values)


def gelu_slope(values):
    return normal_cdf(values) + values * jnp.exp(-0.5 * values * values) * 0.3989422804014327


def segment_table(query_lengths, passage_lengths, total, shift):
    query_starts = jnp.cumsum(query_lengths) - query_lengths
    passage_starts = QTOK + jnp.cumsum(passage_lengths) - passage_lengths
    starts = jnp.concatenate([query_starts, passage_starts])
    lengths = jnp.concatenate([query_lengths, passage_lengths])
    places = ((jnp.arange(total, dtype=jnp.int32) + shift) % total)[:, None]
    inside = (places >= starts[None, :]) & (places < (starts + lengths)[None, :])
    return inside.astype(f32) / lengths.astype(f32)[None, :]


def spread(value, axis, count):
    return lax.all_to_all(jnp.broadcast_to(value[None], (count,) + value.shape), axis, 0, 0)


def other_core(value):
    return lax.ppermute(value, "core", [(0, 1), (1, 0)])


def shifted(value, axis, count, step):
    return lax.ppermute(value, axis, [(j, (j + step) % count) for j in range(count)])


def send_shifted(value, axis, count):
    return [shifted(value, axis, count, k) for k in range(1, count)]


def place_kernel(place, *refs):
    *pieces, out = refs
    count = len(pieces)
    for k, piece in enumerate(pieces):
        out[lax.rem(place[0] + count - k, count)] = piece[...]


def place_pieces(value, moved, axis):
    pieces = [value, *moved]
    vmem = pl.BlockSpec(memory_space=pltpu.VMEM)
    return pl.pallas_call(
        place_kernel,
        out_shape=jax.ShapeDtypeStruct((len(pieces),) + value.shape, value.dtype),
        in_specs=[pl.BlockSpec(memory_space=pltpu.SMEM)] + [vmem] * len(pieces),
        out_specs=vmem,
        compiler_params=pltpu.CompilerParams(vmem_limit_bytes=6 * 1024 * 1024),
        cost_estimate=pl.CostEstimate(flops=0, bytes_accessed=2**21, transcendentals=0),
    )(lax.axis_index(axis).reshape(1).astype(jnp.int32), *pieces)


def sum_permutes(value, axis, count):
    place = lax.axis_index(axis)
    moved = jnp.stack([value] + [shifted(value, axis, count, k) for k in range(1, count)])
    total = lax.dynamic_index_in_dim(moved, place, 0, keepdims=False)
    for k in range(1, count):
        total = total + lax.dynamic_index_in_dim(moved, (place - k) % count, 0, keepdims=False)
    return total


def dot_nt(a, b, precision=None):
    return lax.dot_general(
        a, b, (((1,), (1,)), ((), ())), precision=precision, preferred_element_type=f32
    )


def dot_tn(a, b, precision=None):
    return lax.dot_general(
        a, b, (((0,), (0,)), ((), ())), precision=precision, preferred_element_type=f32
    )


def split_high(value):
    high = value.astype(bf16)
    return high, (value - high.astype(f32)).astype(bf16)


def three_nn(a, high, low):
    a_high, a_low = split_high(a)
    dot = functools.partial(jnp.dot, preferred_element_type=f32)
    return dot(a_high, high[...]) + (dot(a_high, low[...]) + dot(a_low, high[...]))


def loss_kernel(
    scalars, first, second, embed, scale, gain,
    d_logits, loss, d_sums, q_high, q_low, p_high, p_low, logits, times, ids,
):
    core, block = scalars[0], scalars[1]
    half_count = first.shape[0] * 8
    count, width = q_high.shape
    half = width // 2
    listed = ids.shape[0]

    def split(i, carry):
        for source, base in ((first, 0), (second, half_count)):
            rows = pl.ds(pl.multiple_of(base + 16 * i, 16), 16)
            for offset, high, low in ((0, q_high, q_low), (8, p_high, p_low)):
                value = source[pl.ds(2 * i, 2), offset : offset + 8, :width].reshape(16, width)
                high[rows, :], low[rows, :] = split_high(value)
        return carry

    lax.fori_loop(0, half_count // 16, split, 0)
    lanes = [source[:, 0:8, width:].reshape(half_count, 128) for source in (first, second)]
    ids[...] = jnp.concatenate(lanes, axis=0).T[:listed]

    to_logits = 1.0 / (TEMPER * EMBED_STEP * EMBED_STEP)
    raw = dot_nt(p_high[...], q_high[...])
    raw = raw + (dot_nt(p_high[...], q_low[...]) + dot_nt(p_low[...], q_high[...]))
    logits[...] = raw * to_logits

    step = 32
    columns = lax.broadcasted_iota(jnp.int32, (step, count), 1) >> 3
    offsets = lax.broadcasted_iota(jnp.int32, (step, count), 0)

    def fold(value):
        return value.reshape(step // 8, 8, count)

    def count_times(i, carry):
        top, named = carry
        rows = pl.ds(pl.multiple_of(i * step, step), step)
        places = offsets + i * step
        whole = places.astype(f32)
        is_first = whole == ids[0:1, :]
        total = jnp.where(is_first, 1.0, 0.0) + jnp.where((places >> 3) == columns, 1.0, 0.0)
        for k in range(1, listed):
            total = total + jnp.where(whole == ids[k : k + 1, :], 1.0, 0.0)
        value = logits[rows, :]
        times[rows, :] = total
        top = jnp.maximum(top, jnp.max(fold(jnp.where(total > 0.0, value, -1e30)), axis=0))
        return top, named + jnp.sum(fold(jnp.where(is_first, value, 0.0)), axis=0)

    start = (jnp.full((8, count), -1e30, f32), jnp.zeros((8, count), f32))
    top, named = lax.fori_loop(0, count // step, count_times, start)
    top = jnp.max(top, axis=0, keepdims=True)
    named = jnp.sum(named, axis=0, keepdims=True)

    def weigh(i, carry):
        rows = pl.ds(pl.multiple_of(i * step, step), step)
        total = times[rows, :]
        weight = total * jnp.exp(jnp.where(total > 0.0, logits[rows, :] - top, 0.0))
        times[rows, :] = weight
        return carry + jnp.sum(fold(weight), axis=0)

    total = lax.fori_loop(0, count // step, weigh, jnp.zeros((8, count), f32))
    total = jnp.sum(total, axis=0, keepdims=True)
    loss[...] = jnp.broadcast_to(
        jnp.sum(jnp.log(total) + top - named, axis=1, keepdims=True) / count, loss.shape
    )
    share = 1.0 / total

    def differ(i, carry):
        rows = pl.ds(pl.multiple_of(i * step, step), step)
        is_first = (offsets + i * step).astype(f32) == ids[0:1, :]
        d_logits[rows, :] = times[rows, :] * share - jnp.where(is_first, 1.0, 0.0)
        return carry

    lax.fori_loop(0, count // step, differ, 0)

    own_place = block * 8
    picks = lax.broadcasted_iota(jnp.int32, (16, count), 0)
    picks = (lax.broadcasted_iota(jnp.int32, (16, count), 1) == picks + own_place) & (picks < 8)
    picks = jnp.where(picks, 1.0, 0.0).astype(bf16)
    d_high, d_low = split_high(d_logits[...])
    own_queries = dot_nt(picks, d_high) + dot_nt(picks, d_low)
    own_passages = d_logits[pl.ds(pl.multiple_of(own_place, 8), 8), :]
    own_passages = jnp.concatenate([own_passages, jnp.zeros_like(own_passages)], axis=0)
    d_embed = jnp.concatenate(
        [
            three_nn(own_queries, p_high, p_low)[:8],
            three_nn(own_passages, q_high, q_low)[:8],
        ],
        axis=0,
    ) * (1.0 / (TEMPER * EMBED_STEP))
    turned = jnp.concatenate([d_embed[:, half:], d_embed[:, :half]], axis=1)
    d_embed = jnp.where(core == 0, d_embed, turned)
    owned = embed[...]
    inner = jnp.sum(owned * d_embed, axis=1, keepdims=True)
    d_sums[...] = scale[...] * (d_embed - owned * inner) * gain[...]


def back_kernel(
    d_sums, table, own, next1, next2, next3, down_mine, down_theirs, slope,
    d_upward, mine_turned, theirs_turned,
):
    half = mine_turned.shape[0]
    value_high, value_low = split_high(d_sums[...])
    dot = functools.partial(jnp.dot, preferred_element_type=f32)
    for k, source in enumerate((own, next1, next2, next3)):
        size = source.shape[0]
        places = slice(k * size, (k + 1) * size)
        centred = source[...].astype(f32)
        inverse = lax.rsqrt(jnp.mean(centred * centred, axis=1, keepdims=True) + 1e-05)
        normed = centred * inverse
        part_high, part_low = split_high(table[places, :])
        d_normed = dot(part_high, value_high) + (
            dot(part_high, value_low) + dot(part_low, value_high)
        )
        d_mixed = inverse * (
            d_normed
            - jnp.mean(d_normed, axis=1, keepdims=True)
            - normed * jnp.mean(d_normed * normed, axis=1, keepdims=True)
        )
        d_hidden = dot(d_mixed[:, :half].astype(bf16), down_mine[...])
        d_hidden = d_hidden + dot(d_mixed[:, half:].astype(bf16), down_theirs[...])
        d_upward[places, :] = (d_hidden * slope[places, :]).astype(bf16)
        mine_turned[:, places] = d_mixed[:, :half].T.astype(bf16)
        theirs_turned[:, places] = d_mixed[:, half:].T.astype(bf16)


def own_kernel(a, b, c, d, up, down):
    step = 128
    for row in range(0, up.shape[0], step):
        rows = slice(row, row + step)
        up[rows, :] = dot_tn(a[:, rows], b[...])
        down[rows, :] = jnp.dot(c[rows, :], d[...], preferred_element_type=f32)


def other_kernel(up, down, a, b, c, d, out):
    out[0, 0] = (up[...] + dot_tn(a[...], b[...])).astype(bf16)
    out[0, 1] = (down[...] + jnp.dot(c[...], d[...], preferred_element_type=f32)).astype(bf16)


def own_gradients(states, d_upward, d_turned, hidden):
    vmem = pl.BlockSpec(memory_space=pltpu.VMEM)
    shape = jax.ShapeDtypeStruct((d_turned.shape[0], hidden.shape[1]), f32)
    return pl.pallas_call(
        own_kernel,
        out_shape=(shape, shape),
        in_specs=[vmem] * 4,
        out_specs=(vmem, vmem),
        compiler_params=pltpu.CompilerParams(vmem_limit_bytes=12 * 1024 * 1024),
        cost_estimate=pl.CostEstimate(flops=2**31, bytes_accessed=2**16, transcendentals=0),
    )(states, d_upward, d_turned, hidden)


def all_gradients(up, down, states, d_upward, d_turned, hidden):
    step, columns = up.shape[0] // Y, up.shape[1]
    vmem = pl.BlockSpec(memory_space=pltpu.VMEM)
    rows = pl.BlockSpec((step, columns), lambda k: (k, 0))
    return pl.pallas_call(
        other_kernel,
        grid=(Y,),
        out_shape=jax.ShapeDtypeStruct((Y, 2, step, columns), bf16),
        in_specs=[
            rows,
            rows,
            pl.BlockSpec((states.shape[0], step), lambda k: (0, k)),
            vmem,
            pl.BlockSpec((step, d_turned.shape[1]), lambda k: (k, 0)),
            vmem,
        ],
        out_specs=pl.BlockSpec((1, 2, step, columns), lambda k: (k, 0, 0, 0)),
        compiler_params=pltpu.CompilerParams(vmem_limit_bytes=16 * 1024 * 1024),
        cost_estimate=pl.CostEstimate(flops=2**31, bytes_accessed=2**22, transcendentals=0),
    )(up, down, states, d_upward, d_turned, hidden)


def scale_kernel(moved, out):
    owned = out.shape[1] // 2
    width = moved.shape[3]
    for z in range(out.shape[0]):
        for part in range(2):
            rows = slice(z * owned, (z + 1) * owned)
            total = moved[0, part, rows, :].astype(f32)
            for k in range(1, moved.shape[0]):
                total = total + moved[k, part, rows, :].astype(f32)
            largest = jnp.max(jnp.abs(total), axis=1, keepdims=True)
            exponent = jnp.floor(jnp.log(jnp.maximum(largest, 1e-30)) * 1.4426950408889634)
            places = slice(part * owned, (part + 1) * owned)
            out[z, places, :width] = total * jnp.exp(exponent * -0.6931471805599453)
            out[z, places, width:] = jnp.broadcast_to(exponent, (owned, 128))


def scale_rows(moved):
    count, parts, rows, columns = moved.shape
    vmem = pl.BlockSpec(memory_space=pltpu.VMEM)
    return pl.pallas_call(
        scale_kernel,
        out_shape=jax.ShapeDtypeStruct((Z, parts * rows // Z, columns + 128), f32),
        in_specs=[vmem],
        out_specs=vmem,
        compiler_params=pltpu.CompilerParams(vmem_limit_bytes=8 * 1024 * 1024),
        cost_estimate=pl.CostEstimate(flops=2**20, bytes_accessed=2**22, transcendentals=0),
    )(moved)


def all_losses(scalars, first, second, embed, scale, gain, listed):
    count, width = first.shape[0] * 16, embed.shape[1]
    vmem = pl.BlockSpec(memory_space=pltpu.VMEM)
    return pl.pallas_call(
        loss_kernel,
        out_shape=(
            jax.ShapeDtypeStruct((count, count), f32),
            jax.ShapeDtypeStruct((8, 128), f32),
            jax.ShapeDtypeStruct(embed.shape, f32),
        ),
        in_specs=[pl.BlockSpec(memory_space=pltpu.SMEM)] + [vmem] * 5,
        out_specs=(vmem,) * 3,
        scratch_shapes=[pltpu.VMEM((count, width), bf16)] * 4
        + [pltpu.VMEM((count, count), f32)] * 2
        + [pltpu.VMEM((listed, count), f32)],
        compiler_params=pltpu.CompilerParams(vmem_limit_bytes=22 * 1024 * 1024),
        cost_estimate=pl.CostEstimate(flops=2**20, bytes_accessed=2**16, transcendentals=0),
    )(scalars, first, second, embed, scale, gain)


def norm_back(d_sums, table, quarters, down_mine, down_theirs, slope):
    tokens, half = table.shape[0], d_sums.shape[1] // 2
    vmem = pl.BlockSpec(memory_space=pltpu.VMEM)
    return pl.pallas_call(
        back_kernel,
        out_shape=(jax.ShapeDtypeStruct(slope.shape, bf16),)
        + (jax.ShapeDtypeStruct((half, tokens), bf16),) * 2,
        in_specs=[vmem] * (5 + len(quarters)),
        out_specs=(vmem,) * 3,
        compiler_params=pltpu.CompilerParams(vmem_limit_bytes=14 * 1024 * 1024),
        cost_estimate=pl.CostEstimate(flops=2**20, bytes_accessed=2**16, transcendentals=0),
    )(d_sums, table, *quarters, down_mine, down_theirs, slope)


def shards(states, w_up, w_down, gain, query_lengths, passage_lengths, positive, negatives):
    tokens, width = states.shape
    half = width // 2
    owned = w_up.shape[0]
    quarter = tokens // GRP
    queries = positive.shape[0]
    core = lax.axis_index("core")
    member = lax.axis_index("grp")
    block = core * (Y * Z) + lax.axis_index("y") * Z + lax.axis_index("z")

    def swap_halves(value):
        return jnp.where(core == 0, value, jnp.roll(value, half, axis=-1))

    def turn(value):
        parts = value.reshape((GRP, quarter) + value.shape[1:])
        order = [lax.dynamic_index_in_dim(parts, (member + k) % GRP, 0, keepdims=False) for k in range(GRP)]
        return jnp.concatenate(order, axis=0)

    cores = turn(states).reshape(tokens, Y * Z, CORE, owned).transpose(2, 0, 1, 3).reshape(CORE, tokens, half)
    states_mine = lax.dynamic_index_in_dim(cores, core, 0, keepdims=False)
    states_theirs = lax.dynamic_index_in_dim(cores, 1 - core, 0, keepdims=False)
    gain_common = gain.reshape(Y * Z, CORE, owned).transpose(1, 0, 2).reshape(1, width)
    gain_local = swap_halves(gain_common)

    up_z = spread(w_up, "z", Z)
    up_z, states_mine, states_theirs, down_sent = lax.optimization_barrier(
        (up_z, states_mine, states_theirs, w_down.T)
    )
    down_z = spread(down_sent, "z", Z)
    up_moved = send_shifted(up_z, "y", Y)
    up_moved, down_z = lax.optimization_barrier((up_moved, down_z))
    up_mine = place_pieces(up_z, up_moved, "y").reshape(half, -1)
    up_theirs = other_core(up_mine)
    down_moved = send_shifted(down_z, "y", Y)
    states_sent = other_core(states_theirs)

    upward = jnp.dot(states_mine, up_mine, preferred_element_type=f32) + jnp.dot(
        states_theirs, up_theirs, preferred_element_type=f32
    )
    hidden = gelu_exact(upward).astype(bf16)
    hidden, down_moved = lax.optimization_barrier((hidden, down_moved))
    hidden_sent = other_core(hidden)
    down_mine = place_pieces(down_z, down_moved, "y").reshape(half, -1)
    down_theirs = other_core(down_mine)
    down = jnp.concatenate([down_mine, down_theirs], axis=0)

    partial = (dot_nt(hidden[quarter:], down) * PARTIAL_STEP).astype(f16)
    arrived = [
        shifted(partial[(k - 1) * quarter : k * quarter], "grp", GRP, k) for k in range(1, GRP)
    ]
    mixed = jnp.concatenate([states_mine[:quarter], states_theirs[:quarter]], axis=1).astype(f32)
    mixed = mixed + dot_nt(hidden[:quarter], down)
    for piece in arrived:
        mixed = mixed + piece.astype(f32) * (1.0 / PARTIAL_STEP)
    centred = mixed - jnp.mean(mixed, axis=-1, keepdims=True)
    inverse = lax.rsqrt(jnp.mean(centred * centred, axis=-1, keepdims=True) + 1e-05)
    normed = centred * inverse
    table = segment_table(query_lengths[0], passage_lengths[0], tokens, member * quarter)
    pooled = sum_permutes(dot_tn(table[:quarter], normed, EXACT), "grp", GRP) * gain_local
    scale = lax.rsqrt(jnp.sum(pooled * pooled, axis=-1, keepdims=True) + 1e-06)
    embed = pooled * scale

    centred_sent = centred.astype(bf16)
    quarters = [centred_sent] + [shifted(centred_sent, "grp", GRP, GRP - k) for k in range(1, GRP)]
    slope = gelu_slope(upward)

    listed = jnp.concatenate([positive[:, None], negatives], axis=1)
    owner = listed // queries
    listed = ((owner % CORE) * (Y * Z) + owner // CORE) * queries + listed % queries
    lanes = jnp.pad(listed.astype(f32), ((0, queries), (0, 128 - listed.shape[1])))
    sent = jnp.concatenate([swap_halves(embed) * EMBED_STEP, lanes], axis=1).astype(f16)
    mine = spread(sent, "z", Z)
    mine, slope = lax.optimization_barrier((mine, slope))
    mine = spread(mine, "y", Y)
    mine, *quarters = lax.optimization_barrier((mine, *quarters))
    theirs = other_core(mine)
    first = jnp.where(core == 0, mine, theirs).astype(f32).reshape(Y * Z, 2 * queries, width + 128)
    second = jnp.where(core == 0, theirs, mine).astype(f32).reshape(Y * Z, 2 * queries, width + 128)
    d_logits, loss, d_sums = all_losses(
        jnp.stack([core, block]).astype(jnp.int32), first, second, embed, scale, gain_local,
        listed.shape[1],
    )
    d_upward, mine_turned, theirs_turned = norm_back(
        d_sums, table, quarters, down_mine, down_theirs, slope
    )

    d_sent = other_core(theirs_turned)
    d_upward_sent = other_core(d_upward)
    up_own, down_own = own_gradients(states_mine, d_upward, mine_turned, hidden)
    pieces = all_gradients(up_own, down_own, states_sent, d_upward_sent, d_sent, hidden_sent)
    last = scale_rows(lax.all_to_all(pieces, "y", 0, 0)).astype(f16)
    last = lax.all_to_all(last, "z", 0, 0)
    factor = jnp.exp2(last[..., width : width + 1].astype(f32))
    last = jnp.sum(last[..., :width].astype(f32) * factor, axis=0)
    grad_up = last[:owned]
    grad_down = last[owned:].T

    d_logits, first, second, _ = lax.optimization_barrier((d_logits, first, second, pieces))
    both = jnp.concatenate([first, second], axis=0)[:, :, :width]
    all_queries = both[:, :queries].reshape(-1, width) * (1.0 / EMBED_STEP)
    all_passages = both[:, queries:].reshape(-1, width) * (1.0 / EMBED_STEP)
    drawn = jnp.dot(d_logits, all_queries, precision=THREE)
    product = drawn * all_passages
    from_passages = jnp.sum(product, axis=1, keepdims=True)
    from_queries = jnp.sum(
        dot_tn(d_logits, all_passages, THREE) * all_queries, axis=1, keepdims=True
    )
    grad_gain = (
        2.0 * jnp.sum(product, axis=0)
        - jnp.sum(from_queries * all_queries * all_queries, axis=0)
        - jnp.sum(from_passages * all_passages * all_passages, axis=0)
    ) / TEMPER / gain_common[0]
    grad_gain = grad_gain.reshape(CORE, Y * Z, owned).transpose(1, 0, 2).reshape(width)
    return (loss[0, 0], grad_up, grad_down, grad_gain)


def solution(mesh):
    split = Mesh(mesh.devices.reshape(Y, Z, CORE, GRP), ("y", "z", "core", "grp"))
    dp = ("y", "z", "core")
    return jax.shard_map(
        shards,
        mesh=split,
        in_specs=(
            P(dp, None),
            P(dp, "grp"),
            P("grp", dp),
            P(),
            P(dp, None),
            P(dp, None),
            P(dp),
            P(dp, None),
        ),
        out_specs=(P(), P(dp, "grp"), P("grp", dp), P()),
        check_vma=False,
    )
```
